256 devices in a mesh: member: 8 (over z_hi, x), dp: 32 (over z_lo, y, core).
Axes of the slice: x: 4, y: 4, z: 8 (z_hi: 2, z_lo: 4; z = z_hi * 4 + z_lo), core: 2. Of those that a mesh axis runs over, the one named last changes fastest.
Arguments:
- acts: bfloat16 [32, 8, 48, 4096], P('dp', 'member'), may hold values from -6 to 6
- base: bfloat16 [32, 8, 48, 4608], P('dp', 'member'), may hold values from -6 to 6
- down_matrices: bfloat16 [8, 4096, 128], P('member'), may hold values from -0.09375 to 0.09375
- up_matrices: bfloat16 [8, 4608, 128], P('member'), may hold values from -0.5 to 0.5
- head: bfloat16 [8, 4608], P('member'), may hold values from -0.359375 to 0.359375
- gain: float32 [4608], replicated, may hold values from 0.25 to 1.75
- lengths: int32 [32, 4], P('dp'), may hold values from 1 to 192, 384 in all within a row
- pairing: int32 [128], replicated, may hold values from 0 to 127, each once
Outputs:
- loss: float32 [8], P('member')
- grad_a: float32 [8, 4096, 128], P('member', 'dp')
- grad_b: float32 [8, 4608, 128], P('member', 'dp')
The draws below stay inside these ranges and needn't reach their ends.
Inputs may be any that keep to these rules, and one draw needn't show every extreme that they name: Each row of lengths sums to 384; its largest entry is 192. pairing names every response exactly once.
All inputs are finite; a program needn't handle non-finite values.
Results may differ from the reference program's by a relative error of at most 0.0041.
Values may be sent and summed in bfloat16 or wider, within the bound.
A program may use at most 64 MiB of HBM per device.

```python
import math
import jax
import jax.numpy as jnp
import numpy as np
from jax import lax

MODEL_WIDTH = 4608
ATTENTION_WIDTH = 4096
ADAPTER_RANK = 128
TOK_DEV = 48
RESP_DEV = 4
ENSEMBLE_COUNT = 8
SHARD = 384
MOST = 192
RESP = 128
N_MEMBER = 8
N_DP = 32


def block_scale(rng, shape, shards, least, top_value):
    factor_of, own = 1.0, jax.random.fold_in(rng, 6)
    for axis_at, shards_of in shards:
        heights = jnp.exp(jax.random.uniform(jax.random.fold_in(own, axis_at), (shards_of,), jnp.float32, least / len(shards), top_value / len(shards)))
        factor_of = factor_of * jnp.repeat(heights, shape[axis_at] // shards_of).reshape([-1 if axis == axis_at else 1 for axis in range(len(shape))])
    return factor_of


def profile(amount, total, reach, skew):
    portions = [(1 << 20) // math.isqrt(standing ** skew) + 1 for standing in range(2, amount + 1)]
    surplus, given = total - reach - (amount - 1), [1] * (amount - 1)
    while surplus > 0:
        candidates = [i for i in range(amount - 1) if given[i] < reach]
        mass, budget = sum([portions[i] for i in candidates]), surplus
        for i in candidates:
            more = min(reach - given[i], max(1, budget * portions[i] // mass), surplus)
            given[i] = given[i] + more
            surplus = surplus - more
    return np.array([reach] + given)


def uneven(key, amount, total, bound, skew):
    if amount == 2:
        one = jax.random.randint(key, (), max(1, total - bound), min(bound, total - 1) + 1)
        return jnp.stack([one, total - one])
    tallies = jnp.asarray(profile(amount, total, bound, skew), jnp.int32)
    pairs = (amount - 1) // 2
    giver, taker = tallies[1:1 + 2 * pairs:2], tallies[2:2 + 2 * pairs:2]
    room = jnp.minimum(giver - 1, bound - taker)
    passed = jax.random.randint(jax.random.fold_in(key, 1), (pairs,), 0, 1 << 20) % (room + 1)
    tallies = tallies.at[1:1 + 2 * pairs:2].set(giver - passed).at[2:2 + 2 * pairs:2].set(taker + passed)
    return tallies[jax.random.permutation(jax.random.fold_in(key, 2), amount)]


def noise(rng, extent, width, reach, split=(), held_as=jnp.bfloat16):
    result = width * jax.random.normal(rng, extent, jnp.float32)
    if split:
        result = result * block_scale(rng, extent, split, -0.22, 0.18)
    return jnp.clip(result, -reach, reach).astype(held_as)


def setup_inputs(seed: int = 0) -> dict:
    arg_keys = jax.random.split(jax.random.key(seed), 9)
    acts = noise(arg_keys[0], (N_DP, N_MEMBER, TOK_DEV, ATTENTION_WIDTH), 1.0, 6.0, ((0, 32), (1, 8)))
    base = noise(arg_keys[1], (N_DP, N_MEMBER, TOK_DEV, MODEL_WIDTH), 1.0, 6.0, ((0, 32), (1, 8)))
    down_matrices = noise(arg_keys[2], (ENSEMBLE_COUNT, ATTENTION_WIDTH, ADAPTER_RANK), ATTENTION_WIDTH ** -0.5, 0.09375, ((0, 8),))
    up_matrices = noise(arg_keys[3], (ENSEMBLE_COUNT, MODEL_WIDTH, ADAPTER_RANK), ADAPTER_RANK ** -0.5, 0.5, ((0, 8),))
    head = noise(arg_keys[4], (ENSEMBLE_COUNT, MODEL_WIDTH), 0.06, 0.359375, ((0, 8),))
    gain = jnp.clip(1.0 + 0.15 * jax.random.normal(arg_keys[5], (MODEL_WIDTH,), jnp.float32), 0.25, 1.75)
    lengths = jax.vmap(lambda own: uneven(own, RESP_DEV, SHARD, MOST, 2))(jax.random.split(arg_keys[6], N_DP)).reshape((N_DP, RESP_DEV)).astype(jnp.int32)
    pairing = jax.random.permutation(arg_keys[7], RESP).astype(jnp.int32)
    return {"acts": acts, "base": base, "down_matrices": down_matrices, "up_matrices": up_matrices, "head": head, "gain": gain, "lengths": lengths, "pairing": pairing}


def reference(acts, base, down_matrices, up_matrices, head, gain, lengths, pairing):
    shard = N_MEMBER * TOK_DEV
    total_rows = N_DP * shard
    flat_acts = acts.reshape(total_rows, ATTENTION_WIDTH)
    flat_base = base.reshape(total_rows, MODEL_WIDTH).astype(jnp.float32)
    ends = jnp.cumsum(lengths, axis=1).astype(jnp.int32)
    starts = ends - lengths
    position = jnp.arange(shard, dtype=jnp.int32)
    member_of = ((position[None, None, :] >= starts[:, :, None]) & (position[None, None, :] < ends[:, :, None])).astype(jnp.float32)
    inverse_len = 1.0 / lengths.astype(jnp.float32)
    select = (pairing[:, None] == jnp.arange(RESP, dtype=jnp.int32)[None, :]).astype(jnp.float32)
    gain32 = gain.astype(jnp.float32)
    losses = []
    grads_a = []
    grads_b = []
    for member_index in range(ENSEMBLE_COUNT):
        adapter_down = down_matrices[member_index]
        adapter_up = up_matrices[member_index]
        head_vec = head[member_index].astype(jnp.float32)
        low = jnp.dot(flat_acts, adapter_down, preferred_element_type=jnp.float32).astype(jnp.bfloat16)
        y_full = flat_base + lax.dot_general(low, adapter_up, (((1,), (1,)), ((), ())), preferred_element_type=jnp.float32)
        scale = lax.rsqrt(lax.optimization_barrier(jnp.mean(y_full * y_full, axis=1, keepdims=True)) + 1e-06)
        normed = y_full * scale * gain32[None, :]
        score = lax.optimization_barrier(jnp.sum(normed * head_vec[None, :], axis=1)).reshape(N_DP, shard)
        reward = lax.optimization_barrier(jnp.sum(score[:, None, :] * member_of, axis=2)) * inverse_len
        ordered = lax.optimization_barrier(jnp.sum(select * reward.reshape(RESP)[None, :], axis=1))
        margin = ordered[0::2] - ordered[1::2]
        losses.append(jnp.mean(jax.nn.softplus(-margin)))
        slope = -jax.nn.sigmoid(-margin)
        coef = jnp.stack([slope, -slope], axis=1).reshape(RESP)
        dreward = lax.optimization_barrier(jnp.sum(select * coef[:, None], axis=0)).reshape(N_DP, RESP_DEV) * inverse_len
        dscore = lax.optimization_barrier(jnp.sum(dreward[:, :, None] * member_of, axis=1)).reshape(total_rows)
        grad_z = dscore[:, None] * head_vec[None, :] * gain32[None, :]
        inner = lax.optimization_barrier(jnp.mean(grad_z * y_full, axis=1, keepdims=True))
        grad_y = (scale * (grad_z - scale * scale * y_full * inner)).astype(jnp.bfloat16)
        grad_low = jnp.dot(grad_y, adapter_up, preferred_element_type=jnp.float32).astype(jnp.bfloat16)
        grads_a.append(lax.dot_general(flat_acts, grad_low, (((0,), (0,)), ((), ())), preferred_element_type=jnp.float32))
        grads_b.append(lax.dot_general(grad_y, low, (((0,), (0,)), ((), ())), preferred_element_type=jnp.float32))
    return (jnp.stack(losses), jnp.stack(grads_a), jnp.stack(grads_b))
```

```python
import jax
import jax.numpy as jnp
from jax import lax
from jax.experimental import pallas as pl
from jax.experimental.pallas import tpu as pltpu
from jax.sharding import PartitionSpec as P

F32, BF16, I32 = jnp.float32, jnp.bfloat16, jnp.int32
MESH = pl.DeviceIdType.MESH
HIGH = lax.Precision.HIGHEST

NX, NZH, NZL, NY, NC = 4, 2, 4, 4, 2
NZ = NZH * NZL
TOK = 48
ROWS = NX * TOK
AUG = 16
WA, WB, RANK = 4096, 4608, 128
RA, RB = 128, 144
RAB = RA + RB
RESP = 128
XCH = 2
WAB = WA + WB
ZCH = 8
ZROWS = WAB // 4 // ZCH
ZLAG = NZL - 1
TN = (((0,), (0,)), ((), ()))
NT = (((1,), (1,)), ((), ()))


def dot(a, b, dims=(((1,), (0,)), ((), ())), precision=None):
    return lax.dot_general(a, b, dims, precision=precision, preferred_element_type=F32)


def split(v):
    hi = v.astype(BF16)
    return hi, (v - hi.astype(F32)).astype(BF16)


def kernel(
    acts, base, down, up, head, gain, lengths, pairing,
    loss_ref, ga_ref, gb_ref,
    xa, xb, wv, hv, gv, lv, pv, hpk, hrecv, plow, pt, pbh, pnb, gram, rs1, rs2,
    qa, qb, mbd, tmpa, tmpb, g32, gr, rc, b1, s2a, s2b, sa, sb, b2, fin,
    loc, xs, xr, zs, zr, cs, cr, hs, hr, r1s, r1r, r2s, r2r,
    c1s, c1r, y1s, y1r, y2s, y2r, fs, fr,
):
    me_m, me_d = lax.axis_index("member"), lax.axis_index("dp")
    zh, x = lax.div(me_m, NX), lax.rem(me_m, NX)
    zl = lax.div(me_d, NY * NC)
    yc = lax.rem(me_d, NY * NC)
    y, c = lax.div(yc, NC), lax.rem(yc, NC)
    z = zh * NZL + zl

    def dev(x_, z_, yc_):
        return (lax.div(z_, NZL) * NX + x_, lax.rem(z_, NZL) * (NY * NC) + yc_)

    def remote(src, dst, ssem, rsem, to):
        return pltpu.make_async_remote_copy(
            src_ref=src, dst_ref=dst, send_sem=ssem, recv_sem=rsem, device_id=to, device_id_type=MESH
        )

    right, left = lax.rem(x + 1, NX), lax.rem(x + 3, NX)
    zup, zdown, zother = lax.rem(z + 1, NZ), lax.rem(z + 7, NZ), lax.rem(z + 4, NZ)
    core_peer = dev(x, z, y * NC + 1 - c)

    def load(i):
        return pltpu.make_async_copy(*(
            (head, hv), (gain, gv), (lengths, lv), (pairing, pv),
            (acts.at[0, 0], xa.at[pl.ds(0, TOK)]), (base.at[0, 0], xb.at[pl.ds(0, TOK)]),
            (down.at[0], wv.at[0, pl.ds(0, WA)]), (up.at[0], wv.at[0, pl.ds(WA, WB)]),
        )[i], loc.at[i])

    for i in range(8):
        load(i).start()

    barrier = pltpu.get_barrier_semaphore()
    peers = [dev(right, z, yc), dev(left, z, yc)]
    peers += [dev(x, lax.rem(z + d, NZ), yc) for d in range(1, NZ)]
    peers += [dev(x, z, lax.rem(yc + d, NY * NC)) for d in range(1, NY * NC)]
    for peer in peers:
        pl.semaphore_signal(barrier, inc=1, device_id=peer, device_id_type=MESH)
    pl.semaphore_wait(barrier, len(peers))

    ca, cb = WA // XCH, WB // XCH

    def xpiece(i, slot):
        if i < XCH:
            return xa.at[pl.ds(slot * TOK, TOK), pl.ds(i * ca, ca)]
        return xb.at[pl.ds(slot * TOK, TOK), pl.ds((i - XCH) * cb, cb)]

    def xsource(i):
        if i < XCH:
            return acts.at[0, 0, :, pl.ds(i * ca, ca)]
        return base.at[0, 0, :, pl.ds((i - XCH) * cb, cb)]

    def xcopy(i, way):
        if way == 0:
            return remote(xsource(i), xpiece(i, 1), xs.at[0, i], xr.at[0, i], dev(right, z, yc))
        if way == 1:
            return remote(xsource(i), xpiece(i, 2), xs.at[1, i], xr.at[1, i], dev(left, z, yc))
        onward = lax.rem(x + 1 + 2 * c, NX)
        return remote(xpiece(i, 1 + c), xpiece(i, 3), xs.at[2, i], xr.at[2, i], dev(onward, z, yc))

    def xwait(i, way):
        xcopy(i, way).wait_recv()

    def zrows(s, i, core):
        return pl.ds(pl.multiple_of((2 * s + core) * (WAB // 4) + i * ZROWS, 16), ZROWS)

    def zcopy(s, i, own):
        rows = zrows(s, i, c)
        to = zup if s == 0 else zdown
        return remote(wv.at[0 if own else 1, rows], wv.at[1, rows], zs.at[s, i], zr.at[s, i], dev(x, to, yc))

    def ccopy(s, i, core):
        rows = zrows(s, i, core)
        return remote(wv.at[1, rows], wv.at[1, rows], cs.at[s, i], cr.at[s, i], core_peer)

    for i in range(2 * XCH):
        xcopy(i, 0).start()
        xcopy(i, 1).start()
    load(0).wait()
    for i in range(WB // 128):
        hpk[i : i + 1, :] = hv[0:1, i * 128 : (i + 1) * 128].astype(F32)
    hcopy = remote(hpk, hrecv, hs, hr, dev(x, zother, yc))
    hcopy.start()
    load(6).wait()
    load(7).wait()
    edge = (NZL - 1, 0)
    for s in range(2):
        @pl.when(zl == edge[s])
        def _():
            for i in range(ZCH):
                zcopy(s, i, True).start()

    lag = (jnp.maximum(2 * zl - 3, 0), jnp.maximum(3 - 2 * zl, 0))

    def zstep(t, carry):
        for s in range(2):
            i = t - lag[s]

            @pl.when((i >= 0) & (i < ZCH))
            def _():
                zcopy(s, i, False).wait_recv()

                @pl.when(zl != edge[s])
                def _():
                    zcopy(s, i, False).start()

                ccopy(s, i, c).start()

        return carry

    done = 0
    for i in range(2 * XCH):
        until = (5, 7, 9, ZCH + ZLAG)[i]
        lax.fori_loop(done, until, zstep, 0)
        done = until

        @pl.when(c == 0)
        def _():
            xwait(i, 0)

        @pl.when(c == 1)
        def _():
            xwait(i, 1)

        xcopy(i, 2).start()

    hcopy.wait_recv()
    load(1).wait()
    arow = lax.broadcasted_iota(I32, (AUG, 128), 0)
    for i in range(WB // 128):
        cols = slice(i * 128, (i + 1) * 128)
        g = gv[i : i + 1, :]
        hi0, lo0 = split(hpk[i : i + 1, :] * g)
        hi1, lo1 = split(hrecv[i : i + 1, :] * g)
        tile = jnp.where(arow < 2, hi0.astype(F32), 0.0)
        tile = jnp.where(arow == 2, lo0.astype(F32), tile)
        tile = jnp.where((arow == 3) | (arow == 4), hi1.astype(F32), tile)
        tile = jnp.where(arow == 5, lo1.astype(F32), tile)
        xb[ROWS : ROWS + AUG, cols] = tile.astype(BF16)

    for i in (2, 3, 4, 5):
        load(i).wait()

    def cwait(i, carry):
        for s in range(2):
            ccopy(s, i, 1 - c).wait_recv()
        return carry

    lax.fori_loop(0, ZCH, cwait, 0)

    kb = 512
    gram[...] = jnp.zeros_like(gram)

    def wcat(first, n):
        rows = pl.ds(pl.multiple_of(first, 16), n)
        return jnp.concatenate([wv[0, rows, :], wv[1, rows, :]], axis=1)

    def gram_step(i, uh):
        rows = pl.ds(pl.multiple_of(i * kb, kb), kb)
        u = wcat(WA + i * kb, kb)
        gram[...] += dot(u, u, TN)
        return uh + dot(xb[pl.ds(ROWS, AUG), rows], u)

    uh16 = lax.fori_loop(0, WB // kb, gram_step, jnp.zeros((AUG, 2 * RANK), F32))
    lane2 = lax.broadcasted_iota(I32, (1, 2 * RANK), 1)
    uh = jnp.where(lane2 < RANK, uh16[0:1] + uh16[2:3], uh16[3:4] + uh16[5:6])
    same = (lax.broadcasted_iota(I32, (2 * RANK, 2 * RANK), 0) < RANK) == (
        lax.broadcasted_iota(I32, (2 * RANK, 2 * RANK), 1) < RANK
    )
    gram_hi, gram_lo = split(jnp.where(same, gram[...], 0.0))

    def forward(first, n):
        rows = pl.ds(first, n)

        def step_a(i, acc):
            k = pl.ds(pl.multiple_of(i * kb, kb), kb)
            return acc + dot(xa[rows, k], wcat(i * kb, kb))

        plow[rows, :] = lax.fori_loop(0, WA // kb, step_a, jnp.zeros((n, 2 * RANK), F32))

        def step_b(i, acc):
            t, bh, nb = acc
            k = pl.ds(pl.multiple_of(i * kb, kb), kb)
            block = xb[rows, k]
            wide = block.astype(F32)
            square = wide * wide
            for j in range(kb // 128):
                nb = nb + square[:, j * 128 : (j + 1) * 128]
            return (t + dot(block, wcat(WA + i * kb, kb)), bh + dot(block, xb[pl.ds(ROWS, AUG), k], NT), nb)

        t, bh, nb = lax.fori_loop(
            0,
            WB // kb,
            step_b,
            (jnp.zeros((n, 2 * RANK), F32), jnp.zeros((n, AUG), F32), jnp.zeros((n, 128), F32)),
        )
        pt[rows, :] = t
        pbh[rows, :] = bh
        pnb[rows, :] = nb

    for i in range(2 * XCH):
        @pl.when(c == 0)
        def _():
            xwait(i, 1)

        @pl.when(c == 1)
        def _():
            xwait(i, 0)

    forward(0, 3 * TOK)
    for i in range(2 * XCH):
        xwait(i, 2)
    forward(3 * TOK, TOK)

    low = plow[...].astype(BF16)
    lowf = low.astype(F32)
    yu = pt[...] + dot(low, gram_hi) + dot(low, gram_lo)
    cross = lowf * (pt[...] + yu)
    along = lowf * uh
    nb = jnp.sum(pnb[...], axis=1, keepdims=True)
    bh = pbh[...]
    scale, yh = [], []
    for r in range(2):
        half = slice(r * RANK, (r + 1) * RANK)
        n2 = jnp.maximum(nb + jnp.sum(cross[:, half], axis=1, keepdims=True), 0.0)
        scale.append(lax.rsqrt(n2 * (1.0 / WB) + 1e-06))
        yh.append(
            bh[:, 3 * r : 3 * r + 1]
            + bh[:, 3 * r + 2 : 3 * r + 3]
            + jnp.sum(along[:, half], axis=1, keepdims=True)
        )

    row = lax.broadcasted_iota(I32, (ROWS, RESP), 0)
    slot = jnp.where(row < TOK, 0, jnp.where(row < 2 * TOK, 3, jnp.where(row < 3 * TOK, 1, 2)))
    shift = jnp.where(row < TOK, 0, jnp.where(row < 2 * TOK, 1, jnp.where(row < 3 * TOK, 2, 3)))
    block = x + slot
    block = jnp.where(block >= NX, block - NX, block)
    position = zh * ROWS + block * TOK + row - shift * TOK
    lens = [lv[0, k] for k in range(4)]
    lane = lax.broadcasted_iota(I32, (1, RESP), 1) - me_d * 4
    starts = jnp.zeros((1, RESP), I32)
    ends = jnp.zeros((1, RESP), I32)
    counts = jnp.ones((1, RESP), I32)
    begin = 0
    for k in range(4):
        starts = jnp.where(lane == k, begin, starts)
        begin = begin + lens[k]
        ends = jnp.where(lane == k, begin, ends)
        counts = jnp.where(lane == k, lens[k], counts)
    mask = ((position >= starts) & (position < ends)).astype(F32)
    inverse = 1.0 / counts.astype(F32)

    top = lax.broadcasted_iota(I32, (8, RESP), 0)
    part = [jnp.sum(mask * (scale[r] * yh[r]), axis=0, keepdims=True) * inverse for r in range(2)]
    tile = jnp.where(top == 0, part[0], jnp.where(top == 1, part[1], 0.0))

    rs1[yc] = tile
    sends1 = []
    for d in range(1, NY * NC):
        other = lax.rem(yc + d, NY * NC)
        copy = remote(rs1.at[yc], rs1.at[yc], r1s.at[d], r1r.at[yc], dev(x, z, other))
        copy.start()
        sends1.append(copy)
    for d in range(1, NY * NC):
        other = lax.rem(yc + d, NY * NC)
        remote(rs1.at[other], rs1.at[other], r1s.at[d], r1r.at[other], dev(x, z, other)).wait_recv()
    rs2[z] = jnp.sum(rs1[...], axis=0)
    sends2 = []
    for d in range(1, NZ):
        other = lax.rem(z + d, NZ)
        copy = remote(rs2.at[z], rs2.at[z], r2s.at[d], r2r.at[z], dev(x, other, yc))
        copy.start()
        sends2.append(copy)
    for d in range(1, NZ):
        other = lax.rem(z + d, NZ)
        remote(rs2.at[other], rs2.at[other], r2s.at[d], r2r.at[other], dev(x, other, yc)).wait_recv()
    mine = jnp.sum(rs2[pl.ds(zh * NZL, NZL)], axis=0)
    theirs = jnp.sum(rs2[pl.ds((1 - zh) * NZL, NZL)], axis=0)
    rewards = mine + jnp.where(top == 0, theirs[1:2], jnp.where(top == 1, theirs[0:1], 0.0))

    order = pv[0:1, :]
    onehot = (lax.broadcasted_iota(I32, (RESP, RESP), 0) == order).astype(F32)
    ordered = dot(rewards, onehot, precision=HIGH)
    even = lax.rem(lax.broadcasted_iota(I32, (8, RESP), 1), 2) == 0
    margin = jnp.where(
        even, ordered - pltpu.roll(ordered, RESP - 1, 1), pltpu.roll(ordered, 1, 1) - ordered
    )
    soft = jnp.log1p(jnp.exp(-jnp.abs(margin))) + jnp.maximum(-margin, 0.0)
    loss_ref[0] = jnp.sum(jnp.where(even & (top == 0), soft, 0.0)) * (2.0 / RESP)
    slope = 1.0 / (1.0 + jnp.exp(margin))
    coef = jnp.where(even, -slope, slope)
    dreward = dot(coef, onehot, NT, precision=HIGH)

    vrows, crows = [], []
    for r in range(2):
        half = slice(r * RANK, (r + 1) * RANK)
        s = scale[r]
        dscore = jnp.sum(mask * (dreward[r : r + 1] * inverse), axis=1, keepdims=True)
        sd = s * dscore
        cc = s * s * s * (dscore * yh[r] * (1.0 / WB))
        qa[:, half] = (sd * uh[:, half] - cc * yu[:, half]).astype(BF16)
        crow = -cc * lowf[:, half]
        crows.append(crow)
        qb[0:ROWS, half] = crow.astype(BF16)
        vrows.append(jnp.sum(sd * lowf[:, half], axis=0, keepdims=True))
    arow2 = lax.broadcasted_iota(I32, (AUG, RANK), 0)
    for r in range(2):
        hi, lo = split(vrows[r])
        tile = jnp.where((arow2 == 3 * r) | (arow2 == 3 * r + 2), hi.astype(F32), 0.0)
        tile = jnp.where(arow2 == 3 * r + 1, lo.astype(F32), tile)
        qb[ROWS : ROWS + AUG, r * RANK : (r + 1) * RANK] = tile.astype(BF16)
    mbd[...] = jnp.where(same, dot(low, qb[0:ROWS, :], TN), 0.0).astype(BF16)

    def feature_chunk(k):
        return lax.rem(zl + 1 + k, NZL)

    def c1copy(k):
        return remote(gr.at[k], rc.at[k], c1s.at[k], c1r.at[k], core_peer)

    def spread(k, tmp, n, rows):
        for d in range(NY):
            own = tmp[pl.ds(pl.multiple_of((2 * d + c) * n, 16), n), :]
            other = tmp[pl.ds(pl.multiple_of((2 * d + 1 - c) * n, 16), n), :].astype(BF16)
            for r in range(2):
                g32[k, r, d, rows, :] = own[:, r * RANK : (r + 1) * RANK]
                gr[k, r, d, rows, :] = other[:, r * RANK : (r + 1) * RANK]

    def terms(k, carry):
        j = feature_chunk(k)
        for i in range(4):
            cols = pl.ds(pl.multiple_of(j * 1024 + i * 256, 256), 256)
            tmpa[i * 256 : (i + 1) * 256, :] = dot(xa[:, cols], qa[...], TN)
        spread(k, tmpa, RA, slice(0, RA))
        for i in range(3):
            first = j * 1152 + i * 384
            cols = pl.ds(pl.multiple_of(first, 128), 384)
            tmpb[i * 384 : (i + 1) * 384, :] = dot(xb[:, cols], qb[...], TN) + dot(
                wcat(WA + first, 384), mbd[...]
            )
        spread(k, tmpb, RB, slice(RA, RAB))
        c1copy(k).start()
        return carry

    lax.fori_loop(0, NZL, terms, 0)

    ya = y + 1 - 2 * lax.rem(y, 2)
    yb = 3 - y
    cut = (slice(0, RA), slice(RA, RAB))

    def flip(v):
        return v + 1 - 2 * lax.rem(v, 2)

    def sent1(p, i):
        to = (ya, yb)[p]
        return to if i == 0 else ((3 - to) if p == 0 else flip(to))

    def ycopy1(k, p, i):
        dst = (s2a, s2b)[p].at[k, i]
        return remote(
            b1.at[k, :, i, pl.ds(*((0, RA), (RA, RB))[p])],
            dst, y1s.at[k, p, i], y1r.at[k, p, i], dev(x, z, (ya, yb)[p] * NC + c),
        )

    def ycopy2(k, p):
        to = (yb, ya)[p]
        buf = (sa, sb)[p]
        return remote(
            buf.at[0, k], buf.at[1, k], y2s.at[k, p], y2r.at[k, p], dev(x, z, to * NC + c)
        )

    def fcopy(k, r):
        zt = (zh if r == 0 else 1 - zh) * NZL + feature_chunk(k)
        return remote(b2.at[k, r], fin.at[z], fs.at[k, r], fr.at[z], dev(x, zt, yc))

    def step1(k):
        c1copy(k).wait_recv()
        for i in (1, 0):
            for p in range(2):
                chunk = sent1(p, i)
                total = g32[k, :, chunk, cut[p], :] + rc[k, :, chunk, cut[p], :].astype(F32)
                b1[k, :, i, cut[p], :] = total.astype(BF16)
                ycopy1(k, p, i).start()

    def kept(k, p, chunk, i):
        total = g32[k, :, chunk, cut[p], :] + rc[k, :, chunk, cut[p], :].astype(F32)
        return total + (s2a, s2b)[p][k, i].astype(F32)

    def step2(k):
        for p in range(2):
            ycopy1(k, p, 1).wait_recv()
            (sa, sb)[p][0, k] = kept(k, p, (yb, ya)[p], 1).astype(BF16)
            ycopy2(k, p).start()

    def step3(k):
        for p in range(2):
            ycopy1(k, p, 0).wait_recv()
            ycopy2(k, p).wait_recv()
            total = kept(k, p, y, 0) + (sa, sb)[p][1, k].astype(F32)
            b2[k, :, cut[p], :] = total.astype(BF16)
        for r in range(2):
            if k == NZL - 1 and r == 0:
                fin[z] = b2[k, 0]
            else:
                fcopy(k, r).start()

    step1(0)
    step1(1)
    step2(0)
    step1(2)
    step2(1)
    step3(0)
    step1(3)
    step2(2)
    step3(1)
    step2(3)
    step3(2)
    step3(3)
    for d in range(1, NZ):
        other = lax.rem(z + d, NZ)
        remote(b2.at[0, 0], fin.at[other], fs.at[0, 0], fr.at[other], dev(x, other, yc)).wait_recv()
    total = fin[0].astype(F32)
    for i in range(1, NZ):
        total = total + fin[i].astype(F32)
    ga_ref[0] = total[0:RA]
    gb_ref[0] = total[RA:RAB]

    hcopy.wait_send()
    for i in range(2 * XCH):
        for way in range(3):
            xcopy(i, way).wait_send()

    def zdone(i, carry):
        for s in range(2):
            zcopy(s, i, False).wait_send()
            ccopy(s, i, c).wait_send()
        return carry

    lax.fori_loop(0, ZCH, zdone, 0)
    for copy in sends1 + sends2:
        copy.wait_send()
    for k in range(NZL):
        c1copy(k).wait_send()
        for p in range(2):
            for i in range(2):
                ycopy1(k, p, i).wait_send()
            ycopy2(k, p).wait_send()
        for r in range(2):
            if not (k == NZL - 1 and r == 0):
                fcopy(k, r).wait_send()


def per_device(acts, base, down_matrices, up_matrices, head, gain, lengths, pairing):
    hbm = pl.BlockSpec(memory_space=pltpu.HBM)
    vmem = pl.BlockSpec(memory_space=pltpu.VMEM)
    smem = pl.BlockSpec(memory_space=pltpu.SMEM)
    dma = pltpu.SemaphoreType.DMA
    loss, grad_a, grad_b = pl.pallas_call(
        kernel,
        out_shape=(
            jax.ShapeDtypeStruct((1,), F32),
            jax.ShapeDtypeStruct((1, RA, RANK), F32),
            jax.ShapeDtypeStruct((1, RB, RANK), F32),
        ),
        in_specs=[hbm] * 8,
        out_specs=(smem, vmem, vmem),
        scratch_shapes=[
            pltpu.VMEM((ROWS, WA), BF16),
            pltpu.VMEM((ROWS + AUG, WB), BF16),
            pltpu.VMEM((2, WAB, RANK), BF16),
            pltpu.VMEM((1, WB), BF16),
            pltpu.VMEM((WB // 128, 128), F32),
            pltpu.SMEM((1, 4), I32),
            pltpu.VMEM((1, RESP), I32),
            pltpu.VMEM((40, 128), F32),
            pltpu.VMEM((40, 128), F32),
            pltpu.VMEM((ROWS, 2 * RANK), F32),
            pltpu.VMEM((ROWS, 2 * RANK), F32),
            pltpu.VMEM((ROWS, AUG), F32),
            pltpu.VMEM((ROWS, 128), F32),
            pltpu.VMEM((2 * RANK, 2 * RANK), F32),
            pltpu.VMEM((NY * NC, 8, RESP), F32),
            pltpu.VMEM((NZ, 8, RESP), F32),
            pltpu.VMEM((ROWS, 2 * RANK), BF16),
            pltpu.VMEM((ROWS + AUG, 2 * RANK), BF16),
            pltpu.VMEM((2 * RANK, 2 * RANK), BF16),
            pltpu.VMEM((WA // NZL, 2 * RANK), F32),
            pltpu.VMEM((WB // NZL, 2 * RANK), F32),
            pltpu.VMEM((NZL, 2, NY, RAB, RANK), F32),
            pltpu.VMEM((NZL, 2, NY, RAB, RANK), BF16),
            pltpu.VMEM((NZL, 2, NY, RAB, RANK), BF16),
            pltpu.VMEM((NZL, 2, 2, RAB, RANK), BF16),
            pltpu.VMEM((NZL, 2, 2, RA, RANK), BF16),
            pltpu.VMEM((NZL, 2, 2, RB, RANK), BF16),
            pltpu.VMEM((2, NZL, 2, RA, RANK), BF16),
            pltpu.VMEM((2, NZL, 2, RB, RANK), BF16),
            pltpu.VMEM((NZL, 2, RAB, RANK), BF16),
            pltpu.VMEM((NZ, RAB, RANK), BF16),
            dma((8,)),
            dma((3, 2 * XCH)),
            dma((3, 2 * XCH)),
            dma((2, ZCH)),
            dma((2, ZCH)),
            dma((2, ZCH)),
            dma((2, ZCH)),
            dma,
            dma,
            dma((NY * NC,)),
            dma((NY * NC,)),
            dma((NZ,)),
            dma((NZ,)),
            dma((NZL,)),
            dma((NZL,)),
            dma((NZL, 2, 2)),
            dma((NZL, 2, 2)),
            dma((NZL, 2)),
            dma((NZL, 2)),
            dma((NZL, 2)),
            dma((NZ,)),
        ],
        compiler_params=pltpu.CompilerParams(
            collective_id=0, has_side_effects=True, vmem_limit_bytes=60 * 1024 * 1024
        ),
    )(
        acts, base, down_matrices, up_matrices, head,
        gain.reshape(WB // 128, 128), lengths, pairing.reshape(1, RESP),
    )
    return loss, grad_a, grad_b


def solution(mesh):
    return jax.shard_map(
        per_device,
        mesh=mesh,
        in_specs=(
            P("dp", "member", None, None),
            P("dp", "member", None, None),
            P("member", None, None),
            P("member", None, None),
            P("member", None),
            P(),
            P("dp", None),
            P(),
        ),
        out_specs=(P("member"), P("member", "dp", None), P("member", "dp", None)),
        check_vma=False,
    )
```

```python
import jax
import jax.numpy as jnp
from jax import lax
from jax.experimental import pallas as pl
from jax.experimental.pallas import tpu as pltpu
from jax.sharding import PartitionSpec as P

F32, BF16, I32 = jnp.float32, jnp.bfloat16, jnp.int32
MESH = pl.DeviceIdType.MESH

NX, NZH, NZL, NY, NC = 4, 2, 4, 4, 2
NZ = NZH * NZL
TOK = 48
ROWS = NX * TOK
AUG = 16
WA, WB, RANK = 4096, 4608, 128
RA, RB = 128, 144
RAB = RA + RB
RESP = 128
XCH = 2
WAB = WA + WB
WCH = 4
OFFSETS = (0, 1, 3, 2)
TN = (((0,), (0,)), ((), ()))
NT = (((1,), (1,)), ((), ()))


def dot(a, b, dims=(((1,), (0,)), ((), ()))):
    return lax.dot_general(a, b, dims, preferred_element_type=F32)


def split(v):
    hi = v.astype(BF16)
    return hi, (v - hi.astype(F32)).astype(BF16)


def dot3(v, b, dims=(((1,), (0,)), ((), ()))):
    hi = v.astype(BF16)
    rest = v - hi.astype(F32)
    mid = rest.astype(BF16)
    low = (rest - mid.astype(F32)).astype(BF16)
    return dot(hi, b, dims) + dot(mid, b, dims) + dot(low, b, dims)


def kernel(
    acts, base, down, up, head, gain, lengths, pairing,
    loss_ref, ga_ref, gb_ref,
    xa, xb, wv, hv, gv, lv, pv, hpk, hrecv, gram, maskv, apre, cpre, vpre, rs1, rs2,
    lows, qa, qb, mbd, tmpa, tmpb, g32, gr, rc, b1, s2a, s2b, sa, sb, b2, fin,
    loc, xs, xr, zs, zr, ws, wr, cs, cr, hs, hr, r1s, r1r, r2s, r2r,
    c1s, c1r, y1s, y1r, y2s, y2r, fs, fr,
):
    me_m, me_d = lax.axis_index("member"), lax.axis_index("dp")
    zh, x = lax.div(me_m, NX), lax.rem(me_m, NX)
    zl = lax.div(me_d, NY * NC)
    yc = lax.rem(me_d, NY * NC)
    y, c = lax.div(yc, NC), lax.rem(yc, NC)
    z = zh * NZL + zl

    def dev(x_, z_, yc_):
        return (lax.div(z_, NZL) * NX + x_, lax.rem(z_, NZL) * (NY * NC) + yc_)

    def remote(src, dst, ssem, rsem, to):
        return pltpu.make_async_remote_copy(
            src_ref=src, dst_ref=dst, send_sem=ssem, recv_sem=rsem, device_id=to, device_id_type=MESH
        )

    right, left = lax.rem(x + 1, NX), lax.rem(x + 3, NX)
    zother = lax.rem(z + NZL, NZ)
    core_peer = dev(x, z, y * NC + 1 - c)

    def load(i):
        return pltpu.make_async_copy(*(
            (head, hv), (gain, gv), (lengths, lv), (pairing, pv),
            (acts.at[0, 0], xa.at[pl.ds(0, TOK)]), (base.at[0, 0], xb.at[pl.ds(0, TOK)]),
            (down.at[0], wv.at[0, pl.ds(0, WA)]), (up.at[0], wv.at[0, pl.ds(WA, WB)]),
        )[i], loc.at[i])

    for i in range(8):
        load(i).start()

    barrier = pltpu.get_barrier_semaphore()
    peers = [dev(right, z, yc), dev(left, z, yc)]
    peers += [dev(x, lax.rem(z + d, NZ), yc) for d in range(1, NZ)]
    peers += [dev(x, z, lax.rem(yc + d, NY * NC)) for d in range(1, NY * NC)]
    for peer in peers:
        pl.semaphore_signal(barrier, inc=1, device_id=peer, device_id_type=MESH)
    pl.semaphore_wait(barrier, len(peers))

    ca, cb = WA // XCH, WB // XCH

    def xpiece(i, slot):
        if i < XCH:
            return xa.at[pl.ds(slot * TOK, TOK), pl.ds(i * ca, ca)]
        return xb.at[pl.ds(slot * TOK, TOK), pl.ds((i - XCH) * cb, cb)]

    def xsource(i):
        if i < XCH:
            return acts.at[0, 0, :, pl.ds(i * ca, ca)]
        return base.at[0, 0, :, pl.ds((i - XCH) * cb, cb)]

    def xcopy(i, way):
        if way == 0:
            return remote(xsource(i), xpiece(i, 1), xs.at[0, i], xr.at[0, i], dev(right, z, yc))
        if way == 1:
            return remote(xsource(i), xpiece(i, 2), xs.at[1, i], xr.at[1, i], dev(left, z, yc))
        onward = lax.rem(x + 1 + 2 * c, NX)
        return remote(xpiece(i, 1 + c), xpiece(i, 3), xs.at[2, i], xr.at[2, i], dev(onward, z, yc))

    def xwait(i, way):
        xcopy(i, way).wait_recv()

    def wpiece(i, eighth):
        n = (WA if i < WCH // 2 else WB) // (NY * NC) // (WCH // 2)
        first = eighth * (2 * n) + (i % (WCH // 2)) * n
        return pl.multiple_of(first, 16), n

    def wrows(i, eighth):
        first, n = wpiece(i, eighth)
        return wv.at[1, pl.ds(first + (0 if i < WCH // 2 else WA), n)]

    def zcopy(i):
        src = (down if i < WCH // 2 else up).at[0, pl.ds(*wpiece(i, yc))]
        return remote(src, wrows(i, yc), zs.at[i], zr.at[i], dev(x, zother, yc))

    def wcopy(i, d):
        to = lax.rem(y + d, NY)
        return remote(wrows(i, yc), wrows(i, yc), ws.at[d, i], wr.at[d, i], dev(x, z, to * NC + c))

    def wfrom(d, core):
        return lax.rem(y + NY - d, NY) * NC + core

    def ccopy(i, d, core):
        rows = wrows(i, wfrom(d, core))
        return remote(rows, rows, cs.at[d, i], cr.at[d, i], core_peer)

    for i in range(2 * XCH):
        xcopy(i, 0).start()
        xcopy(i, 1).start()
        zcopy(i).start()
    load(0).wait()
    for i in range(WB // 128):
        hpk[i : i + 1, :] = hv[0:1, i * 128 : (i + 1) * 128].astype(F32)
    hcopy = remote(hpk, hrecv, hs, hr, dev(x, zother, yc))
    hcopy.start()

    load(2).wait()
    load(3).wait()
    row = lax.broadcasted_iota(I32, (ROWS, RESP), 0)
    slot = jnp.where(row < TOK, 0, jnp.where(row < 2 * TOK, 3, jnp.where(row < 3 * TOK, 1, 2)))
    shift = jnp.where(row < TOK, 0, jnp.where(row < 2 * TOK, 1, jnp.where(row < 3 * TOK, 2, 3)))
    block = x + slot
    block = jnp.where(block >= NX, block - NX, block)
    position = zh * ROWS + block * TOK + row - shift * TOK
    lens = [lv[0, k] for k in range(4)]
    lane = lax.broadcasted_iota(I32, (1, RESP), 1) - me_d * 4
    starts = jnp.zeros((1, RESP), I32)
    ends = jnp.zeros((1, RESP), I32)
    counts = jnp.ones((1, RESP), I32)
    begin = 0
    for k in range(4):
        starts = jnp.where(lane == k, begin, starts)
        begin = begin + lens[k]
        ends = jnp.where(lane == k, begin, ends)
        counts = jnp.where(lane == k, lens[k], counts)
    inverse = 1.0 / counts.astype(F32)
    maskv[...] = jnp.where((position >= starts) & (position < ends), inverse, 0.0)
    order = jnp.broadcast_to(pv[0:1, :], (8, RESP))
    even8 = lax.rem(lax.broadcasted_iota(I32, (8, RESP), 1), 2) == 0
    swapped = jnp.where(even8, pltpu.roll(order, RESP - 1, 1), pltpu.roll(order, 1, 1))
    number = lax.broadcasted_iota(I32, (RESP, RESP), 0)
    sign = jnp.where(lax.rem(lax.broadcasted_iota(I32, (1, RESP), 1), 2) == 0, 1.0, -1.0)
    onehot = jnp.where(number == order[0:1], sign, 0.0)
    pairs = (onehot - jnp.where(number == swapped[0:1], sign, 0.0)).astype(BF16)
    onehot = onehot.astype(BF16)

    for i in range(2 * XCH):
        zcopy(i).wait_recv()
        for d in range(1, NY):
            wcopy(i, d).start()
        ccopy(i, 0, c).start()

        @pl.when(c == 0)
        def _():
            xwait(i, 0)

        @pl.when(c == 1)
        def _():
            xwait(i, 1)

        xcopy(i, 2).start()

    hcopy.wait_recv()
    load(1).wait()
    arow = lax.broadcasted_iota(I32, (AUG, 128), 0)
    for i in range(WB // 128):
        cols = slice(i * 128, (i + 1) * 128)
        g = gv[i : i + 1, :]
        hi0, lo0 = split(hpk[i : i + 1, :] * g)
        hi1, lo1 = split(hrecv[i : i + 1, :] * g)
        tile = jnp.where(arow < 2, hi0.astype(F32), 0.0)
        tile = jnp.where(arow == 2, lo0.astype(F32), tile)
        tile = jnp.where((arow == 3) | (arow == 4), hi1.astype(F32), tile)
        tile = jnp.where(arow == 5, lo1.astype(F32), tile)
        xb[ROWS : ROWS + AUG, cols] = tile.astype(BF16)

    for i in range(WCH):
        for d in range(1, NY):
            remote(
                wrows(i, wfrom(d, c)), wrows(i, wfrom(d, c)), ws.at[d, i], wr.at[d, i], core_peer
            ).wait_recv()
            ccopy(i, d, c).start()
    for i in (4, 5, 6, 7):
        load(i).wait()
    for i in range(WCH):
        for d in range(NY):
            ccopy(i, d, 1 - c).wait_recv()

    kb = 512
    gram[...] = jnp.zeros_like(gram)

    def wcat(first, n):
        rows = pl.ds(pl.multiple_of(first, 16), n)
        return jnp.concatenate([wv[0, rows, :], wv[1, rows, :]], axis=1)

    def gram_step(i, uh):
        rows = pl.ds(pl.multiple_of(i * kb, kb), kb)
        u = wcat(WA + i * kb, kb)
        gram[...] += dot(u, u, TN)
        return uh + dot(xb[pl.ds(ROWS, AUG), rows], u)

    uh16 = lax.fori_loop(0, WB // kb, gram_step, jnp.zeros((AUG, 2 * RANK), F32))
    lane2 = lax.broadcasted_iota(I32, (1, 2 * RANK), 1)
    uh = jnp.where(lane2 < RANK, uh16[0:1] + uh16[2:3], uh16[3:4] + uh16[5:6])
    same = (lax.broadcasted_iota(I32, (2 * RANK, 2 * RANK), 0) < RANK) == (
        lax.broadcasted_iota(I32, (2 * RANK, 2 * RANK), 1) < RANK
    )
    gram_hi, gram_lo = split(jnp.where(same, gram[...], 0.0))

    top = lax.broadcasted_iota(I32, (8, RESP), 0)

    def forward(first, n):
        rows = pl.ds(first, n)

        def step_a(i, acc):
            k = pl.ds(pl.multiple_of(i * kb, kb), kb)
            return acc + dot(xa[rows, k], wcat(i * kb, kb))

        low = lax.fori_loop(0, WA // kb, step_a, jnp.zeros((n, 2 * RANK), F32)).astype(BF16)

        def step_b(i, acc):
            t, bh, nb = acc
            k = pl.ds(pl.multiple_of(i * kb, kb), kb)
            block = xb[rows, k]
            wide = block.astype(F32)
            square = wide * wide
            for j in range(kb // 128):
                nb = nb + square[:, j * 128 : (j + 1) * 128]
            return (t + dot(block, wcat(WA + i * kb, kb)), bh + dot(block, xb[pl.ds(ROWS, AUG), k], NT), nb)

        t, bh, nb = lax.fori_loop(
            0,
            WB // kb,
            step_b,
            (jnp.zeros((n, 2 * RANK), F32), jnp.zeros((n, AUG), F32), jnp.zeros((n, 128), F32)),
        )
        lows[rows, :] = low
        lowf = low.astype(F32)
        yu = t + dot(low, gram_hi) + dot(low, gram_lo)
        cross = lowf * (t + yu)
        along = lowf * uh
        norm = jnp.sum(nb, axis=1, keepdims=True)
        rewards = []
        for r in range(2):
            half = slice(r * RANK, (r + 1) * RANK)
            n2 = jnp.maximum(norm + jnp.sum(cross[:, half], axis=1, keepdims=True), 0.0)
            s = lax.rsqrt(n2 * (1.0 / WB) + 1e-06)
            yh = (
                bh[:, 3 * r : 3 * r + 1]
                + bh[:, 3 * r + 2 : 3 * r + 3]
                + jnp.sum(along[:, half], axis=1, keepdims=True)
            )
            cc = s * s * s * (yh * (1.0 / WB))
            apre[rows, half] = s * uh[:, half] - cc * yu[:, half]
            cpre[rows, half] = -cc * lowf[:, half]
            vpre[rows, half] = s * lowf[:, half]
            rewards.append(jnp.sum(maskv[rows, :] * (s * yh), axis=0, keepdims=True))
        return jnp.where(top == 0, rewards[0], jnp.where(top == 1, rewards[1], 0.0))

    for i in range(2 * XCH):
        @pl.when(c == 0)
        def _():
            xwait(i, 1)

        @pl.when(c == 1)
        def _():
            xwait(i, 0)

    tile = forward(0, 3 * TOK)
    for i in range(2 * XCH):
        xwait(i, 2)
    tile = tile + forward(3 * TOK, TOK)

    rs1[yc] = tile
    sends1 = []
    for d in range(1, NY * NC):
        other = lax.rem(yc + d, NY * NC)
        copy = remote(rs1.at[yc], rs1.at[yc], r1s.at[d], r1r.at[yc], dev(x, z, other))
        copy.start()
        sends1.append(copy)
    for d in range(1, NY * NC):
        other = lax.rem(yc + d, NY * NC)
        remote(rs1.at[other], rs1.at[other], r1s.at[d], r1r.at[other], dev(x, z, other)).wait_recv()
    rs2[z] = jnp.sum(rs1[...], axis=0)
    sends2 = []
    for d in range(1, NZ):
        other = lax.rem(z + d, NZ)
        copy = remote(rs2.at[z], rs2.at[z], r2s.at[d], r2r.at[z], dev(x, other, yc))
        copy.start()
        sends2.append(copy)
    for d in range(1, NZ):
        other = lax.rem(z + d, NZ)
        remote(rs2.at[other], rs2.at[other], r2s.at[d], r2r.at[other], dev(x, other, yc)).wait_recv()
    mine = jnp.sum(rs2[pl.ds(zh * NZL, NZL)], axis=0)
    theirs = jnp.sum(rs2[pl.ds((1 - zh) * NZL, NZL)], axis=0)
    rewards = mine + jnp.where(top == 0, theirs[1:2], jnp.where(top == 1, theirs[0:1], 0.0))

    margin = dot3(rewards, pairs)
    slope = 1.0 / (1.0 + jnp.exp(margin))
    dreward = -dot3(slope, onehot, NT)
    vrows = []
    for r in range(2):
        half = slice(r * RANK, (r + 1) * RANK)
        dscore = jnp.sum(maskv[...] * dreward[r : r + 1], axis=1, keepdims=True)
        qa[:, half] = (dscore * apre[:, half]).astype(BF16)
        qb[0:ROWS, half] = (dscore * cpre[:, half]).astype(BF16)
        vrows.append(jnp.sum(dscore * vpre[:, half], axis=0, keepdims=True))
    arow2 = lax.broadcasted_iota(I32, (AUG, RANK), 0)
    for r in range(2):
        hi, lo = split(vrows[r])
        tile = jnp.where((arow2 == 3 * r) | (arow2 == 3 * r + 2), hi.astype(F32), 0.0)
        tile = jnp.where(arow2 == 3 * r + 1, lo.astype(F32), tile)
        qb[ROWS : ROWS + AUG, r * RANK : (r + 1) * RANK] = tile.astype(BF16)
    mbd[...] = jnp.where(same, dot(lows[...], qb[0:ROWS, :], TN), 0.0).astype(BF16)

    def feature_chunk(k):
        return lax.rem(zl + OFFSETS[k], NZL)

    def c1copy(k):
        return remote(gr.at[k], rc.at[k], c1s.at[k], c1r.at[k], core_peer)

    def spread(k, tmp, n, rows):
        for d in range(NY):
            own = tmp[pl.ds(pl.multiple_of((2 * d + c) * n, 16), n), :]
            other = tmp[pl.ds(pl.multiple_of((2 * d + 1 - c) * n, 16), n), :].astype(BF16)
            for r in range(2):
                g32[k, r, d, rows, :] = own[:, r * RANK : (r + 1) * RANK]
                gr[k, r, d, rows, :] = other[:, r * RANK : (r + 1) * RANK]

    def terms(k):
        j = feature_chunk(k)
        for i in range(4):
            cols = pl.ds(pl.multiple_of(j * 1024 + i * 256, 256), 256)
            tmpa[i * 256 : (i + 1) * 256, :] = dot(xa[:, cols], qa[...], TN)
        spread(k, tmpa, RA, slice(0, RA))
        for i in range(3):
            first = j * 1152 + i * 384
            cols = pl.ds(pl.multiple_of(first, 128), 384)
            tmpb[i * 384 : (i + 1) * 384, :] = dot(xb[:, cols], qb[...], TN) + dot(
                wcat(WA + first, 384), mbd[...]
            )
        spread(k, tmpb, RB, slice(RA, RAB))
        c1copy(k).start()

    ya = y + 1 - 2 * lax.rem(y, 2)
    yb = 3 - y
    cut = (slice(0, RA), slice(RA, RAB))

    def flip(v):
        return v + 1 - 2 * lax.rem(v, 2)

    def sent1(p, i):
        to = (ya, yb)[p]
        return to if i == 0 else ((3 - to) if p == 0 else flip(to))

    def ycopy1(k, p, i):
        dst = (s2a, s2b)[p].at[k, i]
        return remote(
            b1.at[k, :, i, pl.ds(*((0, RA), (RA, RB))[p])],
            dst, y1s.at[k, p, i], y1r.at[k, p, i], dev(x, z, (ya, yb)[p] * NC + c),
        )

    def ycopy2(k, p):
        to = (yb, ya)[p]
        buf = (sa, sb)[p]
        return remote(
            buf.at[0, k], buf.at[1, k], y2s.at[k, p], y2r.at[k, p], dev(x, z, to * NC + c)
        )

    def fcopy(k, r):
        zt = (zh if r == 0 else 1 - zh) * NZL + feature_chunk(k)
        return remote(b2.at[k, r], fin.at[z], fs.at[k, r], fr.at[z], dev(x, zt, yc))

    def step1(k):
        c1copy(k).wait_recv()
        for i in (1, 0):
            for p in range(2):
                chunk = sent1(p, i)
                total = g32[k, :, chunk, cut[p], :] + rc[k, :, chunk, cut[p], :].astype(F32)
                b1[k, :, i, cut[p], :] = total.astype(BF16)
                ycopy1(k, p, i).start()

    def kept(k, p, chunk, i):
        total = g32[k, :, chunk, cut[p], :] + rc[k, :, chunk, cut[p], :].astype(F32)
        return total + (s2a, s2b)[p][k, i].astype(F32)

    def step2(k):
        for p in range(2):
            ycopy1(k, p, 1).wait_recv()
            (sa, sb)[p][0, k] = kept(k, p, (yb, ya)[p], 1).astype(BF16)
            ycopy2(k, p).start()

    def step3(k):
        for p in range(2):
            ycopy1(k, p, 0).wait_recv()
            ycopy2(k, p).wait_recv()
            total = kept(k, p, y, 0) + (sa, sb)[p][1, k].astype(F32)
            b2[k, :, cut[p], :] = total.astype(BF16)
        for r in range(2):
            if k == 0 and r == 0:
                fin[z] = b2[k, 0]
            else:
                fcopy(k, r).start()

    terms(0)
    terms(1)
    step1(0)
    terms(2)
    step1(1)
    terms(3)
    step1(2)
    step2(0)
    step1(3)
    step2(1)
    step3(0)
    soft = jnp.log1p(jnp.exp(-jnp.abs(margin))) + jnp.maximum(-margin, 0.0)
    loss_ref[0] = jnp.sum(jnp.where(even8 & (top == 0), soft, 0.0)) * (2.0 / RESP)
    step2(2)
    step3(1)
    step2(3)
    step3(2)
    step3(3)
    for d in range(1, NZ):
        other = lax.rem(z + d, NZ)
        remote(b2.at[0, 0], fin.at[other], fs.at[0, 0], fr.at[other], dev(x, other, yc)).wait_recv()
    total = fin[0].astype(F32)
    for i in range(1, NZ):
        total = total + fin[i].astype(F32)
    ga_ref[0] = total[0:RA]
    gb_ref[0] = total[RA:RAB]

    hcopy.wait_send()
    for i in range(2 * XCH):
        for way in range(3):
            xcopy(i, way).wait_send()

    for i in range(WCH):
        zcopy(i).wait_send()
        for d in range(NY):
            ccopy(i, d, c).wait_send()
            if d:
                wcopy(i, d).wait_send()
    for copy in sends1 + sends2:
        copy.wait_send()
    for k in range(NZL):
        c1copy(k).wait_send()
        for p in range(2):
            for i in range(2):
                ycopy1(k, p, i).wait_send()
            ycopy2(k, p).wait_send()
        for r in range(2):
            if not (k == 0 and r == 0):
                fcopy(k, r).wait_send()


def per_device(acts, base, down_matrices, up_matrices, head, gain, lengths, pairing):
    hbm = pl.BlockSpec(memory_space=pltpu.HBM)
    vmem = pl.BlockSpec(memory_space=pltpu.VMEM)
    smem = pl.BlockSpec(memory_space=pltpu.SMEM)
    dma = pltpu.SemaphoreType.DMA
    loss, grad_a, grad_b = pl.pallas_call(
        kernel,
        out_shape=(
            jax.ShapeDtypeStruct((1,), F32),
            jax.ShapeDtypeStruct((1, RA, RANK), F32),
            jax.ShapeDtypeStruct((1, RB, RANK), F32),
        ),
        in_specs=[hbm] * 8,
        out_specs=(smem, vmem, vmem),
        scratch_shapes=[
            pltpu.VMEM((ROWS, WA), BF16),
            pltpu.VMEM((ROWS + AUG, WB), BF16),
            pltpu.VMEM((2, WAB, RANK), BF16),
            pltpu.VMEM((1, WB), BF16),
            pltpu.VMEM((WB // 128, 128), F32),
            pltpu.SMEM((1, 4), I32),
            pltpu.VMEM((1, RESP), I32),
            pltpu.VMEM((40, 128), F32),
            pltpu.VMEM((40, 128), F32),
            pltpu.VMEM((2 * RANK, 2 * RANK), F32),
            pltpu.VMEM((ROWS, RESP), F32),
            pltpu.VMEM((ROWS, 2 * RANK), F32),
            pltpu.VMEM((ROWS, 2 * RANK), F32),
            pltpu.VMEM((ROWS, 2 * RANK), F32),
            pltpu.VMEM((NY * NC, 8, RESP), F32),
            pltpu.VMEM((NZ, 8, RESP), F32),
            pltpu.VMEM((ROWS, 2 * RANK), BF16),
            pltpu.VMEM((ROWS, 2 * RANK), BF16),
            pltpu.VMEM((ROWS + AUG, 2 * RANK), BF16),
            pltpu.VMEM((2 * RANK, 2 * RANK), BF16),
            pltpu.VMEM((WA // NZL, 2 * RANK), F32),
            pltpu.VMEM((WB // NZL, 2 * RANK), F32),
            pltpu.VMEM((NZL, 2, NY, RAB, RANK), F32),
            pltpu.VMEM((NZL, 2, NY, RAB, RANK), BF16),
            pltpu.VMEM((NZL, 2, NY, RAB, RANK), BF16),
            pltpu.VMEM((NZL, 2, 2, RAB, RANK), BF16),
            pltpu.VMEM((NZL, 2, 2, RA, RANK), BF16),
            pltpu.VMEM((NZL, 2, 2, RB, RANK), BF16),
            pltpu.VMEM((2, NZL, 2, RA, RANK), BF16),
            pltpu.VMEM((2, NZL, 2, RB, RANK), BF16),
            pltpu.VMEM((NZL, 2, RAB, RANK), BF16),
            pltpu.VMEM((NZ, RAB, RANK), BF16),
            dma((8,)),
            dma((3, 2 * XCH)),
            dma((3, 2 * XCH)),
            dma((WCH,)),
            dma((WCH,)),
            dma((NY, WCH)),
            dma((NY, WCH)),
            dma((NY, WCH)),
            dma((NY, WCH)),
            dma,
            dma,
            dma((NY * NC,)),
            dma((NY * NC,)),
            dma((NZ,)),
            dma((NZ,)),
            dma((NZL,)),
            dma((NZL,)),
            dma((NZL, 2, 2)),
            dma((NZL, 2, 2)),
            dma((NZL, 2)),
            dma((NZL, 2)),
            dma((NZL, 2)),
            dma((NZ,)),
        ],
        compiler_params=pltpu.CompilerParams(
            collective_id=0, has_side_effects=True, vmem_limit_bytes=60 * 1024 * 1024
        ),
    )(
        acts, base, down_matrices, up_matrices, head,
        gain.reshape(WB // 128, 128), lengths, pairing.reshape(1, RESP),
    )
    return loss, grad_a, grad_b


def solution(mesh):
    return jax.shard_map(
        per_device,
        mesh=mesh,
        in_specs=(
            P("dp", "member", None, None),
            P("dp", "member", None, None),
            P("member", None, None),
            P("member", None, None),
            P("member", None),
            P(),
            P("dp", None),
            P(),
        ),
        out_specs=(P("member"), P("member", "dp", None), P("member", "dp", None)),
        check_vma=False,
    )
```

```python
import jax
import jax.numpy as jnp
from jax import lax
from jax.experimental import pallas as pl
from jax.experimental.pallas import tpu as pltpu
from jax.sharding import PartitionSpec as P

F32, BF16, I32 = jnp.float32, jnp.bfloat16, jnp.int32
MESH = pl.DeviceIdType.MESH

NX, NZH, NZL, NY, NC = 4, 2, 4, 4, 2
NZ = NZH * NZL
TOK = 48
ROWS = NX * TOK
AUG = 16
WA, WB, RANK = 4096, 4608, 128
RA, RB = 128, 144
RAB = RA + RB
RESP = 128
XCH = 2
WAB = WA + WB
WCH = 4
OFFSETS = (1, 3, 2, 0)
UNITS = [(k, r if k < NZL - 1 else 1 - r) for k in range(NZL) for r in range(2)]
KA, KB = 512, 768
TN = (((0,), (0,)), ((), ()))
NT = (((1,), (1,)), ((), ()))


def dot(a, b, dims=(((1,), (0,)), ((), ()))):
    return lax.dot_general(a, b, dims, preferred_element_type=F32)


def split(v):
    hi = v.astype(BF16)
    return hi, (v - hi.astype(F32)).astype(BF16)


def dot3(v, b, dims=(((1,), (0,)), ((), ()))):
    hi = v.astype(BF16)
    rest = v - hi.astype(F32)
    mid = rest.astype(BF16)
    low = (rest - mid.astype(F32)).astype(BF16)
    return dot(hi, b, dims) + dot(mid, b, dims) + dot(low, b, dims)


def kernel(
    acts, base, down, up, head, gain, lengths, pairing,
    loss_ref, out_ref,
    xa, xb, wv, hv, gv, lv, pv, hpk, hrecv, gram, maskv, apre, cpre, vpre, rs1, rs2,
    lows, qa, qb, mbd, tmpa, tmpb, g32, gr, rc, b1, s2a, s2b, sa, sb, b2, fin,
    loc, xs, xr, zs, zr, ws, wr, cs, cr, hs, hr, r1s, r1r, r2s, r2r,
    c1s, c1r, y1s, y1r, y2s, y2r, fs, fr,
):
    me_m, me_d = lax.axis_index("member"), lax.axis_index("dp")
    zh, x = lax.div(me_m, NX), lax.rem(me_m, NX)
    zl = lax.div(me_d, NY * NC)
    yc = lax.rem(me_d, NY * NC)
    y, c = lax.div(yc, NC), lax.rem(yc, NC)
    z = zh * NZL + zl

    def dev(x_, z_, yc_):
        return (lax.div(z_, NZL) * NX + x_, lax.rem(z_, NZL) * (NY * NC) + yc_)

    def remote(src, dst, ssem, rsem, to):
        return pltpu.make_async_remote_copy(
            src_ref=src, dst_ref=dst, send_sem=ssem, recv_sem=rsem, device_id=to, device_id_type=MESH
        )

    right, left = lax.rem(x + 1, NX), lax.rem(x + 3, NX)
    zother = lax.rem(z + NZL, NZ)
    core_peer = dev(x, z, y * NC + 1 - c)

    def load(i):
        return pltpu.make_async_copy(*(
            (head, hv), (gain, gv), (lengths, lv), (pairing, pv),
            (acts.at[0, 0], xa.at[pl.ds(0, TOK)]), (base.at[0, 0], xb.at[pl.ds(0, TOK)]),
            (down.at[0], wv.at[0, pl.ds(0, WA)]), (up.at[0], wv.at[0, pl.ds(WA, WB)]),
        )[i], loc.at[i])

    for i in range(8):
        load(i).start()

    barrier = pltpu.get_barrier_semaphore()
    peers = [dev(right, z, yc), dev(left, z, yc)]
    peers += [dev(x, lax.rem(z + d, NZ), yc) for d in range(1, NZ)]
    peers += [dev(x, z, lax.rem(yc + d, NY * NC)) for d in range(1, NY * NC)]
    for peer in peers:
        pl.semaphore_signal(barrier, inc=1, device_id=peer, device_id_type=MESH)
    pl.semaphore_wait(barrier, len(peers))

    ca, cb = WA // XCH, WB // XCH

    def xpiece(i, slot):
        if i < XCH:
            return xa.at[pl.ds(slot * TOK, TOK), pl.ds(i * ca, ca)]
        return xb.at[pl.ds(slot * TOK, TOK), pl.ds((i - XCH) * cb, cb)]

    def xsource(i):
        if i < XCH:
            return acts.at[0, 0, :, pl.ds(i * ca, ca)]
        return base.at[0, 0, :, pl.ds((i - XCH) * cb, cb)]

    def xcopy(i, way):
        if way == 0:
            return remote(xsource(i), xpiece(i, 1), xs.at[0, i], xr.at[0, i], dev(right, z, yc))
        if way == 1:
            return remote(xsource(i), xpiece(i, 2), xs.at[1, i], xr.at[1, i], dev(left, z, yc))
        onward = lax.rem(x + 1 + 2 * c, NX)
        return remote(xpiece(i, 1 + c), xpiece(i, 3), xs.at[2, i], xr.at[2, i], dev(onward, z, yc))

    def xwait(i, way):
        xcopy(i, way).wait_recv()

    def wpiece(i, eighth):
        n = (WA if i < WCH // 2 else WB) // (NY * NC) // (WCH // 2)
        first = eighth * (2 * n) + (i % (WCH // 2)) * n
        return pl.multiple_of(first, 16), n

    def wrows(i, eighth):
        first, n = wpiece(i, eighth)
        return wv.at[1, pl.ds(first + (0 if i < WCH // 2 else WA), n)]

    def zcopy(i):
        src = (down if i < WCH // 2 else up).at[0, pl.ds(*wpiece(i, yc))]
        return remote(src, wrows(i, yc), zs.at[i], zr.at[i], dev(x, zother, yc))

    def wcopy(i, d):
        to = lax.rem(y + d, NY)
        return remote(wrows(i, yc), wrows(i, yc), ws.at[d, i], wr.at[d, i], dev(x, z, to * NC + c))

    def wfrom(d, core):
        return lax.rem(y + NY - d, NY) * NC + core

    def ccopy(i, d, core):
        rows = wrows(i, wfrom(d, core))
        return remote(rows, rows, cs.at[d, i], cr.at[d, i], core_peer)

    for i in range(2 * XCH):
        xcopy(i, 0).start()
        xcopy(i, 1).start()
        zcopy(i).start()
    load(0).wait()
    for i in range(WB // 128):
        hpk[i : i + 1, :] = hv[0:1, i * 128 : (i + 1) * 128].astype(F32)
    hcopy = remote(hpk, hrecv, hs, hr, dev(x, zother, yc))
    hcopy.start()

    load(2).wait()
    load(3).wait()
    row = lax.broadcasted_iota(I32, (ROWS, RESP), 0)
    slot = jnp.where(row < TOK, 0, jnp.where(row < 2 * TOK, 3, jnp.where(row < 3 * TOK, 1, 2)))
    shift = jnp.where(row < TOK, 0, jnp.where(row < 2 * TOK, 1, jnp.where(row < 3 * TOK, 2, 3)))
    block = x + slot
    block = jnp.where(block >= NX, block - NX, block)
    position = zh * ROWS + block * TOK + row - shift * TOK
    lens = [lv[0, k] for k in range(4)]
    lane = lax.broadcasted_iota(I32, (1, RESP), 1) - me_d * 4
    starts = jnp.zeros((1, RESP), I32)
    ends = jnp.zeros((1, RESP), I32)
    counts = jnp.ones((1, RESP), I32)
    begin = 0
    for k in range(4):
        starts = jnp.where(lane == k, begin, starts)
        begin = begin + lens[k]
        ends = jnp.where(lane == k, begin, ends)
        counts = jnp.where(lane == k, lens[k], counts)
    inverse = 1.0 / counts.astype(F32)
    maskv[...] = jnp.where((position >= starts) & (position < ends), inverse, 0.0)
    order = jnp.broadcast_to(pv[0:1, :], (8, RESP))
    even8 = lax.rem(lax.broadcasted_iota(I32, (8, RESP), 1), 2) == 0
    swapped = jnp.where(even8, pltpu.roll(order, RESP - 1, 1), pltpu.roll(order, 1, 1))
    number = lax.broadcasted_iota(I32, (RESP, RESP), 0)
    sign = jnp.where(lax.rem(lax.broadcasted_iota(I32, (1, RESP), 1), 2) == 0, 1.0, -1.0)
    onehot = jnp.where(number == order[0:1], sign, 0.0)
    pairs = (onehot - jnp.where(number == swapped[0:1], sign, 0.0)).astype(BF16)
    onehot = onehot.astype(BF16)

    for i in range(2 * XCH):
        zcopy(i).wait_recv()
        for d in range(1, NY):
            wcopy(i, d).start()
        ccopy(i, 0, c).start()

        @pl.when(c == 0)
        def _():
            xwait(i, 0)

        @pl.when(c == 1)
        def _():
            xwait(i, 1)

        xcopy(i, 2).start()

    hcopy.wait_recv()
    load(1).wait()
    arow = lax.broadcasted_iota(I32, (AUG, 128), 0)
    for i in range(WB // 128):
        cols = slice(i * 128, (i + 1) * 128)
        g = gv[i : i + 1, :]
        hi0, lo0 = split(hpk[i : i + 1, :] * g)
        hi1, lo1 = split(hrecv[i : i + 1, :] * g)
        tile = jnp.where(arow < 2, hi0.astype(F32), 0.0)
        tile = jnp.where(arow == 2, lo0.astype(F32), tile)
        tile = jnp.where((arow == 3) | (arow == 4), hi1.astype(F32), tile)
        tile = jnp.where(arow == 5, lo1.astype(F32), tile)
        xb[ROWS : ROWS + AUG, cols] = tile.astype(BF16)

    for i in range(WCH):
        for d in range(1, NY):
            remote(
                wrows(i, wfrom(d, c)), wrows(i, wfrom(d, c)), ws.at[d, i], wr.at[d, i], core_peer
            ).wait_recv()
            ccopy(i, d, c).start()
    for i in (4, 5, 6, 7):
        load(i).wait()
    for i in range(WCH):
        for d in range(NY):
            ccopy(i, d, 1 - c).wait_recv()

    gram[...] = jnp.zeros_like(gram)

    def wcat(first, n):
        rows = pl.ds(pl.multiple_of(first, 16), n)
        return jnp.concatenate([wv[0, rows, :], wv[1, rows, :]], axis=1)

    def gram_step(i, uh):
        rows = pl.ds(pl.multiple_of(i * KB, KB), KB)
        u = wcat(WA + i * KB, KB)
        gram[...] += dot(u, u, TN)
        return uh + dot(xb[pl.ds(ROWS, AUG), rows], u)

    uh16 = lax.fori_loop(0, WB // KB, gram_step, jnp.zeros((AUG, 2 * RANK), F32))
    lane2 = lax.broadcasted_iota(I32, (1, 2 * RANK), 1)
    uh = jnp.where(lane2 < RANK, uh16[0:1] + uh16[2:3], uh16[3:4] + uh16[5:6])
    same = (lax.broadcasted_iota(I32, (2 * RANK, 2 * RANK), 0) < RANK) == (
        lax.broadcasted_iota(I32, (2 * RANK, 2 * RANK), 1) < RANK
    )
    gram_hi, gram_lo = split(jnp.where(same, gram[...], 0.0))

    top = lax.broadcasted_iota(I32, (8, RESP), 0)

    def forward_a(first, n, begin, end, acc):
        rows = pl.ds(first, n)

        def step(i, acc):
            k = pl.ds(pl.multiple_of(i * KA, KA), KA)
            return acc + dot(xa[rows, k], wcat(i * KA, KA))

        return lax.fori_loop(begin, end, step, acc)

    def forward_b(first, n, begin, end, acc):
        rows = pl.ds(first, n)

        def step(i, acc):
            t, bh, nb = acc
            k = pl.ds(pl.multiple_of(i * KB, KB), KB)
            block = xb[rows, k]
            wide = block.astype(F32)
            square = wide * wide
            for j in range(KB // 128):
                nb = nb + square[:, j * 128 : (j + 1) * 128]
            return (
                t + dot(block, wcat(WA + i * KB, KB)),
                bh + dot(block, xb[pl.ds(ROWS, AUG), k], NT),
                nb,
            )

        return lax.fori_loop(begin, end, step, acc)

    def nothing(n):
        return jnp.zeros((n, 2 * RANK), F32), (
            jnp.zeros((n, 2 * RANK), F32), jnp.zeros((n, AUG), F32), jnp.zeros((n, 128), F32),
        )

    def scores(first, n, low32, acc):
        rows = pl.ds(first, n)
        low = low32.astype(BF16)
        t, bh, nb = acc
        lows[rows, :] = low
        lowf = low.astype(F32)
        yu = t + dot(low, gram_hi) + dot(low, gram_lo)
        cross = lowf * (t + yu)
        along = lowf * uh
        norm = jnp.sum(nb, axis=1, keepdims=True)
        rewards = []
        for r in range(2):
            half = slice(r * RANK, (r + 1) * RANK)
            n2 = jnp.maximum(norm + jnp.sum(cross[:, half], axis=1, keepdims=True), 0.0)
            s = lax.rsqrt(n2 * (1.0 / WB) + 1e-06)
            yh = (
                bh[:, 3 * r : 3 * r + 1]
                + bh[:, 3 * r + 2 : 3 * r + 3]
                + jnp.sum(along[:, half], axis=1, keepdims=True)
            )
            cc = s * s * s * (yh * (1.0 / WB))
            apre[rows, half] = s * uh[:, half] - cc * yu[:, half]
            cpre[rows, half] = -cc * lowf[:, half]
            vpre[rows, half] = s * lowf[:, half]
            rewards.append(jnp.sum(maskv[rows, :] * (s * yh), axis=0, keepdims=True))
        return jnp.where(top == 0, rewards[0], jnp.where(top == 1, rewards[1], 0.0))

    for i in range(2 * XCH):
        @pl.when(c == 0)
        def _():
            xwait(i, 1)

        @pl.when(c == 1)
        def _():
            xwait(i, 0)

    acc_a, acc_b = nothing(3 * TOK)
    acc_a = forward_a(0, 3 * TOK, 0, WA // KA, acc_a)
    acc_b = forward_b(0, 3 * TOK, 0, WB // KB, acc_b)
    tile = scores(0, 3 * TOK, acc_a, acc_b)
    acc_a, acc_b = nothing(TOK)
    na, nb = WA // KA // XCH, WB // KB // XCH
    for i in range(XCH):
        xwait(i, 2)
        acc_a = forward_a(3 * TOK, TOK, i * na, (i + 1) * na, acc_a)
    for i in range(XCH):
        xwait(XCH + i, 2)
        acc_b = forward_b(3 * TOK, TOK, i * nb, (i + 1) * nb, acc_b)
    tile = tile + scores(3 * TOK, TOK, acc_a, acc_b)

    rs1[yc] = tile
    sends1 = []
    for d in range(1, NY * NC):
        other = lax.rem(yc + d, NY * NC)
        copy = remote(rs1.at[yc], rs1.at[yc], r1s.at[d], r1r.at[yc], dev(x, z, other))
        copy.start()
        sends1.append(copy)
    for d in range(1, NY * NC):
        other = lax.rem(yc + d, NY * NC)
        remote(rs1.at[other], rs1.at[other], r1s.at[d], r1r.at[other], dev(x, z, other)).wait_recv()
    rs2[z] = jnp.sum(rs1[...], axis=0)
    sends2 = []
    for d in range(1, NZ):
        other = lax.rem(z + d, NZ)
        copy = remote(rs2.at[z], rs2.at[z], r2s.at[d], r2r.at[z], dev(x, other, yc))
        copy.start()
        sends2.append(copy)
    for d in range(1, NZ):
        other = lax.rem(z + d, NZ)
        remote(rs2.at[other], rs2.at[other], r2s.at[d], r2r.at[other], dev(x, other, yc)).wait_recv()
    mine = jnp.sum(rs2[pl.ds(zh * NZL, NZL)], axis=0)
    theirs = jnp.sum(rs2[pl.ds((1 - zh) * NZL, NZL)], axis=0)
    rewards = mine + jnp.where(top == 0, theirs[1:2], jnp.where(top == 1, theirs[0:1], 0.0))

    margin = dot3(rewards, pairs)
    slope = 1.0 / (1.0 + jnp.exp(margin))
    dreward = -dot3(slope, onehot, NT)
    vrows = []
    for r in range(2):
        half = slice(r * RANK, (r + 1) * RANK)
        dscore = jnp.sum(maskv[...] * dreward[r : r + 1], axis=1, keepdims=True)
        qa[:, half] = (dscore * apre[:, half]).astype(BF16)
        qb[0:ROWS, half] = (dscore * cpre[:, half]).astype(BF16)
        vrows.append(jnp.sum(dscore * vpre[:, half], axis=0, keepdims=True))
    arow2 = lax.broadcasted_iota(I32, (AUG, RANK), 0)
    for r in range(2):
        hi, lo = split(vrows[r])
        tile = jnp.where((arow2 == 3 * r) | (arow2 == 3 * r + 2), hi.astype(F32), 0.0)
        tile = jnp.where(arow2 == 3 * r + 1, lo.astype(F32), tile)
        qb[ROWS : ROWS + AUG, r * RANK : (r + 1) * RANK] = tile.astype(BF16)
    mbd[...] = jnp.where(same, dot(lows[...], qb[0:ROWS, :], TN), 0.0).astype(BF16)

    def feature_chunk(k):
        return lax.rem(zl + OFFSETS[k], NZL)

    def c1copy(k, r):
        return remote(gr.at[k, r], rc.at[k, r], c1s.at[k, r], c1r.at[k, r], core_peer)

    def spread(k, tmp, n, rows):
        for d in range(NY):
            own = tmp[pl.ds(pl.multiple_of((2 * d + c) * n, 16), n), :]
            other = tmp[pl.ds(pl.multiple_of((2 * d + 1 - c) * n, 16), n), :].astype(BF16)
            for r in range(2):
                g32[k, r, d, rows, :] = own[:, r * RANK : (r + 1) * RANK]
                gr[k, r, d, rows, :] = other[:, r * RANK : (r + 1) * RANK]

    def terms(k):
        j = feature_chunk(k)
        for i in range(4):
            cols = pl.ds(pl.multiple_of(j * 1024 + i * 256, 256), 256)
            tmpa[i * 256 : (i + 1) * 256, :] = dot(xa[:, cols], qa[...], TN)
        spread(k, tmpa, RA, slice(0, RA))
        for i in range(3):
            first = j * 1152 + i * 384
            cols = pl.ds(pl.multiple_of(first, 128), 384)
            tmpb[i * 384 : (i + 1) * 384, :] = dot(xb[:, cols], qb[...], TN) + dot(
                wcat(WA + first, 384), mbd[...]
            )
        spread(k, tmpb, RB, slice(RA, RAB))
        for kk, r in UNITS:
            if kk == k:
                c1copy(k, r).start()

    ya = y + 1 - 2 * lax.rem(y, 2)
    yb = 3 - y
    cut = (slice(0, RA), slice(RA, RAB))

    def flip(v):
        return v + 1 - 2 * lax.rem(v, 2)

    def sent1(p, i):
        to = (ya, yb)[p]
        return to if i == 0 else ((3 - to) if p == 0 else flip(to))

    def ycopy1(k, r, p, i):
        u = 2 * k + r
        return remote(
            b1.at[k, r, i, pl.ds(*((0, RA), (RA, RB))[p])], (s2a, s2b)[p].at[k, r, i],
            y1s.at[u, p, i], y1r.at[u, p, i], dev(x, z, (ya, yb)[p] * NC + c),
        )

    def ycopy2(k, r, p):
        u = 2 * k + r
        buf = (sa, sb)[p]
        return remote(
            buf.at[0, k, r], buf.at[1, k, r],
            y2s.at[u, p], y2r.at[u, p], dev(x, z, (yb, ya)[p] * NC + c),
        )

    def fcopy(k, r):
        zt = (zh if r == 0 else 1 - zh) * NZL + feature_chunk(k)
        return remote(b2.at[k, r], fin.at[z], fs.at[k, r], fr.at[z], dev(x, zt, yc))

    def coresum(k, r, p, chunk):
        return g32[k, r, chunk, cut[p], :] + rc[k, r, chunk, cut[p], :].astype(F32)

    def step1(k, r):
        c1copy(k, r).wait_recv()
        for i in (1, 0):
            for p in range(2):
                b1[k, r, i, cut[p], :] = coresum(k, r, p, sent1(p, i)).astype(BF16)
                ycopy1(k, r, p, i).start()

    def kept(k, r, p, chunk, i):
        return coresum(k, r, p, chunk) + (s2a, s2b)[p][k, r, i].astype(F32)

    def step2(k, r):
        for p in range(2):
            ycopy1(k, r, p, 1).wait_recv()
            (sa, sb)[p][0, k, r] = kept(k, r, p, (yb, ya)[p], 1).astype(BF16)
            ycopy2(k, r, p).start()

    def step3(k, r):
        for p in range(2):
            ycopy1(k, r, p, 0).wait_recv()
            ycopy2(k, r, p).wait_recv()
            total = kept(k, r, p, y, 0) + (sa, sb)[p][1, k, r].astype(F32)
            b2[k, r, cut[p], :] = total.astype(BF16)
        if (k, r) == UNITS[-1]:
            fin[z] = b2[k, r]
        else:
            fcopy(k, r).start()

    terms(0)
    terms(1)
    for u in range(len(UNITS) + 4):
        if u < len(UNITS):
            step1(*UNITS[u])
        if u in (1, 3):
            terms((u + 3) // 2)
        if 2 <= u < len(UNITS) + 2:
            step2(*UNITS[u - 2])
        if u >= 4:
            step3(*UNITS[u - 4])
        if u == len(UNITS) // 2:
            soft = jnp.log1p(jnp.exp(-jnp.abs(margin))) + jnp.maximum(-margin, 0.0)
            loss_ref[0] = jnp.sum(jnp.where(even8 & (top == 0), soft, 0.0)) * (2.0 / RESP)
    for d in range(1, NZ):
        other = lax.rem(z + d, NZ)
        remote(b2.at[0, 0], fin.at[other], fs.at[0, 0], fr.at[other], dev(x, other, yc)).wait_recv()
    total = fin[0].astype(F32)
    for i in range(1, NZ):
        total = total + fin[i].astype(F32)
    out_ref[...] = total

    hcopy.wait_send()
    for i in range(2 * XCH):
        for way in range(3):
            xcopy(i, way).wait_send()

    for i in range(WCH):
        zcopy(i).wait_send()
        for d in range(NY):
            ccopy(i, d, c).wait_send()
            if d:
                wcopy(i, d).wait_send()
    for copy in sends1 + sends2:
        copy.wait_send()
    for k, r in UNITS:
        c1copy(k, r).wait_send()
        for p in range(2):
            for i in range(2):
                ycopy1(k, r, p, i).wait_send()
            ycopy2(k, r, p).wait_send()
        if (k, r) != UNITS[-1]:
            fcopy(k, r).wait_send()


def divide(whole, ga, gb):
    ga[0] = whole[0:RA]
    gb[0] = whole[RA:RAB]


def per_device(acts, base, down_matrices, up_matrices, head, gain, lengths, pairing):
    hbm = pl.BlockSpec(memory_space=pltpu.HBM)
    vmem = pl.BlockSpec(memory_space=pltpu.VMEM)
    smem = pl.BlockSpec(memory_space=pltpu.SMEM)
    dma = pltpu.SemaphoreType.DMA
    loss, whole = pl.pallas_call(
        kernel,
        out_shape=(
            jax.ShapeDtypeStruct((1,), F32),
            jax.ShapeDtypeStruct((RAB, RANK), F32),
        ),
        in_specs=[hbm] * 8,
        out_specs=(smem, vmem),
        scratch_shapes=[
            pltpu.VMEM((ROWS, WA), BF16),
            pltpu.VMEM((ROWS + AUG, WB), BF16),
            pltpu.VMEM((2, WAB, RANK), BF16),
            pltpu.VMEM((1, WB), BF16),
            pltpu.VMEM((WB // 128, 128), F32),
            pltpu.SMEM((1, 4), I32),
            pltpu.VMEM((1, RESP), I32),
            pltpu.VMEM((40, 128), F32),
            pltpu.VMEM((40, 128), F32),
            pltpu.VMEM((2 * RANK, 2 * RANK), F32),
            pltpu.VMEM((ROWS, RESP), F32),
            pltpu.VMEM((ROWS, 2 * RANK), F32),
            pltpu.VMEM((ROWS, 2 * RANK), F32),
            pltpu.VMEM((ROWS, 2 * RANK), F32),
            pltpu.VMEM((NY * NC, 8, RESP), F32),
            pltpu.VMEM((NZ, 8, RESP), F32),
            pltpu.VMEM((ROWS, 2 * RANK), BF16),
            pltpu.VMEM((ROWS, 2 * RANK), BF16),
            pltpu.VMEM((ROWS + AUG, 2 * RANK), BF16),
            pltpu.VMEM((2 * RANK, 2 * RANK), BF16),
            pltpu.VMEM((WA // NZL, 2 * RANK), F32),
            pltpu.VMEM((WB // NZL, 2 * RANK), F32),
            pltpu.VMEM((NZL, 2, NY, RAB, RANK), F32),
            pltpu.VMEM((NZL, 2, NY, RAB, RANK), BF16),
            pltpu.VMEM((NZL, 2, NY, RAB, RANK), BF16),
            pltpu.VMEM((NZL, 2, 2, RAB, RANK), BF16),
            pltpu.VMEM((NZL, 2, 2, RA, RANK), BF16),
            pltpu.VMEM((NZL, 2, 2, RB, RANK), BF16),
            pltpu.VMEM((2, NZL, 2, RA, RANK), BF16),
            pltpu.VMEM((2, NZL, 2, RB, RANK), BF16),
            pltpu.VMEM((NZL, 2, RAB, RANK), BF16),
            pltpu.VMEM((NZ, RAB, RANK), BF16),
            dma((8,)),
            dma((3, 2 * XCH)),
            dma((3, 2 * XCH)),
            dma((WCH,)),
            dma((WCH,)),
            dma((NY, WCH)),
            dma((NY, WCH)),
            dma((NY, WCH)),
            dma((NY, WCH)),
            dma,
            dma,
            dma((NY * NC,)),
            dma((NY * NC,)),
            dma((NZ,)),
            dma((NZ,)),
            dma((NZL, 2)),
            dma((NZL, 2)),
            dma((2 * NZL, 2, 2)),
            dma((2 * NZL, 2, 2)),
            dma((2 * NZL, 2)),
            dma((2 * NZL, 2)),
            dma((NZL, 2)),
            dma((NZ,)),
        ],
        compiler_params=pltpu.CompilerParams(
            collective_id=0, has_side_effects=True, vmem_limit_bytes=60 * 1024 * 1024
        ),
    )(
        acts, base, down_matrices, up_matrices, head,
        gain.reshape(WB // 128, 128), lengths, pairing.reshape(1, RESP),
    )
    grad_a, grad_b = pl.pallas_call(
        divide,
        out_shape=(
            jax.ShapeDtypeStruct((1, RA, RANK), F32),
            jax.ShapeDtypeStruct((1, RB, RANK), F32),
        ),
        in_specs=[vmem],
        out_specs=(vmem, vmem),
    )(whole)
    return loss, grad_a, grad_b


def solution(mesh):
    return jax.shard_map(
        per_device,
        mesh=mesh,
        in_specs=(
            P("dp", "member", None, None),
            P("dp", "member", None, None),
            P("member", None, None),
            P("member", None, None),
            P("member", None),
            P(),
            P("dp", None),
            P(),
        ),
        out_specs=(P("member"), P("member", "dp", None), P("member", "dp", None)),
        check_vma=False,
    )
```

```python
import jax
import jax.numpy as jnp
from jax import lax
from jax.experimental import pallas as pl
from jax.experimental.pallas import tpu as pltpu
from jax.sharding import PartitionSpec as P

F32, BF16, I32 = jnp.float32, jnp.bfloat16, jnp.int32
MESH = pl.DeviceIdType.MESH

NX, NZH, NZL, NY, NC = 4, 2, 4, 4, 2
NZ = NZH * NZL
TOK = 48
ROWS = NX * TOK
AUG = 16
WA, WB, RANK = 4096, 4608, 128
RA, RB = 128, 144
RAB = RA + RB
RESP = 128
XA, XB = 2, 6
XP = XA + XB
WAB = WA + WB
WCH = 4
OFFSETS = (0, 3, 1, 2)
UNITS = ((0, 4), (1, 3), (2, -3), (3, 2), (3, -2), (2, 1), (1, -1), (0, 0))
KA, KB = 512, 768
TN = (((0,), (0,)), ((), ()))
NT = (((1,), (1,)), ((), ()))


def dot(a, b, dims=(((1,), (0,)), ((), ()))):
    return lax.dot_general(a, b, dims, preferred_element_type=F32)


def split(v):
    hi = v.astype(BF16)
    return hi, (v - hi.astype(F32)).astype(BF16)


def dot3(v, b, dims=(((1,), (0,)), ((), ()))):
    hi = v.astype(BF16)
    rest = v - hi.astype(F32)
    mid = rest.astype(BF16)
    low = (rest - mid.astype(F32)).astype(BF16)
    return dot(hi, b, dims) + dot(mid, b, dims) + dot(low, b, dims)


def kernel(
    acts, base, down, up, head, gain, lengths, pairing,
    out_ref,
    xa, xb, wv, hv, gv, lv, pv, hpk, hrecv, gram, maskv, apre, cpre, vpre, rs1, rs2,
    lows, qa, qb, mbd, tmpa, tmpb, g32, gr, rc, b1, s2a, s2b, sa, sb, b2, fin,
    loc, xs, xr, zs, zr, ws, wr, cs, cr, hs, hr, r1s, r1r, r2s, r2r,
    c1s, c1r, y1s, y1r, y2s, y2r, fs, fr,
):
    me_m, me_d = lax.axis_index("member"), lax.axis_index("dp")
    zh, x = lax.div(me_m, NX), lax.rem(me_m, NX)
    zl = lax.div(me_d, NY * NC)
    yc = lax.rem(me_d, NY * NC)
    y, c = lax.div(yc, NC), lax.rem(yc, NC)
    z = zh * NZL + zl

    def dev(x_, z_, yc_):
        return (lax.div(z_, NZL) * NX + x_, lax.rem(z_, NZL) * (NY * NC) + yc_)

    def remote(src, dst, ssem, rsem, to):
        return pltpu.make_async_remote_copy(
            src_ref=src, dst_ref=dst, send_sem=ssem, recv_sem=rsem, device_id=to, device_id_type=MESH
        )

    right, left = lax.rem(x + 1, NX), lax.rem(x + 3, NX)
    zother = lax.rem(z + NZL, NZ)
    core_peer = dev(x, z, y * NC + 1 - c)

    def load(i):
        return pltpu.make_async_copy(*(
            (head, hv), (gain, gv), (lengths, lv), (pairing, pv),
            (acts.at[0, 0], xa.at[pl.ds(0, TOK)]), (base.at[0, 0], xb.at[pl.ds(0, TOK)]),
            (down.at[0], wv.at[0, pl.ds(0, WA)]), (up.at[0], wv.at[0, pl.ds(WA, WB)]),
        )[i], loc.at[i])

    for i in range(8):
        load(i).start()

    barrier = pltpu.get_barrier_semaphore()
    peers = [dev(right, z, yc), dev(left, z, yc)]
    peers += [dev(x, lax.rem(z + d, NZ), yc) for d in range(1, NZ)]
    peers += [dev(x, z, lax.rem(yc + d, NY * NC)) for d in range(1, NY * NC)]
    for peer in peers:
        pl.semaphore_signal(barrier, inc=1, device_id=peer, device_id_type=MESH)
    pl.semaphore_wait(barrier, len(peers))

    ca, cb = WA // XA, WB // XB

    def xpiece(i, slot):
        if i < XA:
            return xa.at[pl.ds(slot * TOK, TOK), pl.ds(i * ca, ca)]
        return xb.at[pl.ds(slot * TOK, TOK), pl.ds((i - XA) * cb, cb)]

    def xsource(i):
        if i < XA:
            return acts.at[0, 0, :, pl.ds(i * ca, ca)]
        return base.at[0, 0, :, pl.ds((i - XA) * cb, cb)]

    def xcopy(i, way):
        if way == 0:
            return remote(xsource(i), xpiece(i, 1), xs.at[0, i], xr.at[0, i], dev(right, z, yc))
        if way == 1:
            return remote(xsource(i), xpiece(i, 2), xs.at[1, i], xr.at[1, i], dev(left, z, yc))
        turn = c if i < XA else 1 - c
        onward = lax.rem(x + 1 + 2 * turn, NX)
        return remote(xpiece(i, 1 + turn), xpiece(i, 3), xs.at[2, i], xr.at[2, i], dev(onward, z, yc))

    def xwait(i, way):
        xcopy(i, way).wait_recv()

    def xwait_side(i, onward):
        first = 0 if (i < XA) == onward else 1

        @pl.when(c == 0)
        def _():
            xwait(i, first)

        @pl.when(c == 1)
        def _():
            xwait(i, 1 - first)

    def wpiece(i, eighth):
        n = (WA if i < WCH // 2 else WB) // (NY * NC) // (WCH // 2)
        first = eighth * (2 * n) + (i % (WCH // 2)) * n
        return pl.multiple_of(first, 16), n

    def wrows(i, eighth):
        first, n = wpiece(i, eighth)
        return wv.at[1, pl.ds(first + (0 if i < WCH // 2 else WA), n)]

    def zcopy(i):
        src = (down if i < WCH // 2 else up).at[0, pl.ds(*wpiece(i, yc))]
        return remote(src, wrows(i, yc), zs.at[i], zr.at[i], dev(x, zother, yc))

    def wcopy(i, d):
        to = lax.rem(y + d, NY)
        return remote(wrows(i, yc), wrows(i, yc), ws.at[d, i], wr.at[d, i], dev(x, z, to * NC + c))

    def wfrom(d, core):
        return lax.rem(y + NY - d, NY) * NC + core

    def ccopy(i, d, core):
        rows = wrows(i, wfrom(d, core))
        return remote(rows, rows, cs.at[d, i], cr.at[d, i], core_peer)

    for i in range(XP):
        xcopy(i, 0).start()
        xcopy(i, 1).start()
        if i < WCH:
            zcopy(i).start()
    load(0).wait()
    for i in range(WB // 128):
        hpk[i : i + 1, :] = hv[0:1, i * 128 : (i + 1) * 128].astype(F32)
    hcopy = remote(hpk, hrecv, hs, hr, dev(x, zother, yc))
    hcopy.start()

    load(2).wait()
    load(3).wait()
    row = lax.broadcasted_iota(I32, (ROWS, RESP), 0)
    slot = jnp.where(row < TOK, 0, jnp.where(row < 2 * TOK, 3, jnp.where(row < 3 * TOK, 1, 2)))
    shift = jnp.where(row < TOK, 0, jnp.where(row < 2 * TOK, 1, jnp.where(row < 3 * TOK, 2, 3)))
    block = x + slot
    block = jnp.where(block >= NX, block - NX, block)
    position = zh * ROWS + block * TOK + row - shift * TOK
    lens = [lv[0, k] for k in range(4)]
    lane = lax.broadcasted_iota(I32, (1, RESP), 1) - me_d * 4
    starts = jnp.zeros((1, RESP), I32)
    ends = jnp.zeros((1, RESP), I32)
    counts = jnp.ones((1, RESP), I32)
    begin = 0
    for k in range(4):
        starts = jnp.where(lane == k, begin, starts)
        begin = begin + lens[k]
        ends = jnp.where(lane == k, begin, ends)
        counts = jnp.where(lane == k, lens[k], counts)
    inverse = 1.0 / counts.astype(F32)
    maskv[...] = jnp.where((position >= starts) & (position < ends), inverse, 0.0)
    order = jnp.broadcast_to(pv[0:1, :], (8, RESP))
    even8 = lax.rem(lax.broadcasted_iota(I32, (8, RESP), 1), 2) == 0
    swapped = jnp.where(even8, pltpu.roll(order, RESP - 1, 1), pltpu.roll(order, 1, 1))
    number = lax.broadcasted_iota(I32, (RESP, RESP), 0)
    sign = jnp.where(lax.rem(lax.broadcasted_iota(I32, (1, RESP), 1), 2) == 0, 1.0, -1.0)
    onehot = jnp.where(number == order[0:1], sign, 0.0)
    pairs = (onehot - jnp.where(number == swapped[0:1], sign, 0.0)).astype(BF16)
    onehot = onehot.astype(BF16)

    for i in range(XP):
        if i < WCH:
            zcopy(i).wait_recv()
            for d in range(1, NY):
                wcopy(i, d).start()
            ccopy(i, 0, c).start()
        xwait_side(i, True)
        xcopy(i, 2).start()

    hcopy.wait_recv()
    load(1).wait()
    arow = lax.broadcasted_iota(I32, (AUG, 128), 0)
    for i in range(WB // 128):
        cols = slice(i * 128, (i + 1) * 128)
        g = gv[i : i + 1, :]
        hi0, lo0 = split(hpk[i : i + 1, :] * g)
        hi1, lo1 = split(hrecv[i : i + 1, :] * g)
        tile = jnp.where(arow < 2, hi0.astype(F32), 0.0)
        tile = jnp.where(arow == 2, lo0.astype(F32), tile)
        tile = jnp.where((arow == 3) | (arow == 4), hi1.astype(F32), tile)
        tile = jnp.where(arow == 5, lo1.astype(F32), tile)
        xb[ROWS : ROWS + AUG, cols] = tile.astype(BF16)

    def share(pieces):
        for i in pieces:
            for d in range(1, NY):
                remote(
                    wrows(i, wfrom(d, c)), wrows(i, wfrom(d, c)), ws.at[d, i], wr.at[d, i], core_peer
                ).wait_recv()
                ccopy(i, d, c).start()

    def shared(pieces):
        for i in pieces:
            for d in range(NY):
                ccopy(i, d, 1 - c).wait_recv()

    def wcat(first, n):
        rows = pl.ds(pl.multiple_of(first, 16), n)
        return jnp.concatenate([wv[0, rows, :], wv[1, rows, :]], axis=1)

    def forward_a(first, n, begin, end, acc):
        rows = pl.ds(first, n)

        def step(i, acc):
            k = pl.ds(pl.multiple_of(i * KA, KA), KA)
            return acc + dot(xa[rows, k], wcat(i * KA, KA))

        return lax.fori_loop(begin, end, step, acc)

    def nothing(n):
        return jnp.zeros((n, 2 * RANK), F32), (
            jnp.zeros((n, 2 * RANK), F32), jnp.zeros((n, AUG), F32), jnp.zeros((n, 128), F32),
        )

    for i in (4, 5, 6, 7):
        load(i).wait()
    share(range(WCH // 2))
    shared(range(WCH // 2))
    for i in range(XA):
        xwait_side(i, False)
    near_a, near_b = nothing(3 * TOK)
    near_a = forward_a(0, 3 * TOK, 0, WA // KA, near_a)
    share(range(WCH // 2, WCH))
    shared(range(WCH // 2, WCH))

    gram[...] = jnp.zeros_like(gram)

    def gram_step(i, uh):
        rows = pl.ds(pl.multiple_of(i * KB, KB), KB)
        u = wcat(WA + i * KB, KB)
        gram[...] += dot(u, u, TN)
        return uh + dot(xb[pl.ds(ROWS, AUG), rows], u)

    uh16 = lax.fori_loop(0, WB // KB, gram_step, jnp.zeros((AUG, 2 * RANK), F32))
    lane2 = lax.broadcasted_iota(I32, (1, 2 * RANK), 1)
    uh = jnp.where(lane2 < RANK, uh16[0:1] + uh16[2:3], uh16[3:4] + uh16[5:6])
    same = (lax.broadcasted_iota(I32, (2 * RANK, 2 * RANK), 0) < RANK) == (
        lax.broadcasted_iota(I32, (2 * RANK, 2 * RANK), 1) < RANK
    )
    gram_hi, gram_lo = split(jnp.where(same, gram[...], 0.0))

    top = lax.broadcasted_iota(I32, (8, RESP), 0)

    def forward_b(first, n, begin, end, acc):
        rows = pl.ds(first, n)

        def step(i, acc):
            t, bh, nb = acc
            k = pl.ds(pl.multiple_of(i * KB, KB), KB)
            block = xb[rows, k]
            wide = block.astype(F32)
            square = wide * wide
            for j in range(KB // 128):
                nb = nb + square[:, j * 128 : (j + 1) * 128]
            return (
                t + dot(block, wcat(WA + i * KB, KB)),
                bh + dot(block, xb[pl.ds(ROWS, AUG), k], NT),
                nb,
            )

        return lax.fori_loop(begin, end, step, acc)

    def early(low32, rows):
        low = low32.astype(BF16)
        lowf = low.astype(F32)
        lows[rows, :] = low
        along = lowf * uh
        return lowf, dot(low, gram_hi) + dot(low, gram_lo), [
            jnp.sum(along[:, r * RANK : (r + 1) * RANK], axis=1, keepdims=True) for r in range(2)
        ]

    def scores(rows, before, acc):
        lowf, lowg, along = before
        t, bh, nb = acc
        yu = t + lowg
        cross = lowf * (t + yu)
        norm = jnp.sum(nb, axis=1, keepdims=True)
        rewards = []
        for r in range(2):
            half = slice(r * RANK, (r + 1) * RANK)
            n2 = jnp.maximum(norm + jnp.sum(cross[:, half], axis=1, keepdims=True), 0.0)
            s = lax.rsqrt(n2 * (1.0 / WB) + 1e-06)
            yh = (
                bh[:, 3 * r : 3 * r + 1]
                + bh[:, 3 * r + 2 : 3 * r + 3]
                + along[r]
            )
            cc = s * s * s * (yh * (1.0 / WB))
            apre[rows, half] = s * uh[:, half] - cc * yu[:, half]
            cpre[rows, half] = -cc * lowf[:, half]
            vpre[rows, half] = s * lowf[:, half]
            rewards.append(jnp.sum(maskv[rows, :] * (s * yh), axis=0, keepdims=True))
        return jnp.where(top == 0, rewards[0], jnp.where(top == 1, rewards[1], 0.0))

    for i in range(XA, XP):
        xwait_side(i, False)
    near_b = forward_b(0, 3 * TOK, 0, WB // KB, near_b)
    near = pl.ds(0, 3 * TOK)
    tile = scores(near, early(near_a, near), near_b)
    far_a, far_b = nothing(TOK)
    na, nb = WA // KA // XA, WB // KB // XB
    for i in range(XA):
        xwait(i, 2)
        far_a = forward_a(3 * TOK, TOK, i * na, (i + 1) * na, far_a)
    far = pl.ds(3 * TOK, TOK)
    before = early(far_a, far)
    for i in range(XB):
        xwait(XA + i, 2)
        far_b = forward_b(3 * TOK, TOK, i * nb, (i + 1) * nb, far_b)
    tile = tile + scores(far, before, far_b)

    rs1[yc] = tile
    sends1 = []
    for d in range(1, NY * NC):
        other = lax.rem(yc + d, NY * NC)
        copy = remote(rs1.at[yc], rs1.at[yc], r1s.at[d], r1r.at[yc], dev(x, z, other))
        copy.start()
        sends1.append(copy)
    hcopy.wait_send()
    for i in range(XP):
        for way in range(3):
            xcopy(i, way).wait_send()

    for i in range(WCH):
        zcopy(i).wait_send()
        for d in range(NY):
            ccopy(i, d, c).wait_send()
            if d:
                wcopy(i, d).wait_send()
    for d in range(1, NY * NC):
        other = lax.rem(yc + d, NY * NC)
        remote(rs1.at[other], rs1.at[other], r1s.at[d], r1r.at[other], dev(x, z, other)).wait_recv()
    rs2[z] = jnp.sum(rs1[...], axis=0)
    sends2 = []
    for d in range(1, NZ):
        other = lax.rem(z + d, NZ)
        copy = remote(rs2.at[z], rs2.at[z], r2s.at[d], r2r.at[z], dev(x, other, yc))
        copy.start()
        sends2.append(copy)
    for d in range(1, NZ):
        other = lax.rem(z + d, NZ)
        remote(rs2.at[other], rs2.at[other], r2s.at[d], r2r.at[other], dev(x, other, yc)).wait_recv()
    mine = jnp.sum(rs2[pl.ds(zh * NZL, NZL)], axis=0)
    theirs = jnp.sum(rs2[pl.ds((1 - zh) * NZL, NZL)], axis=0)
    rewards = mine + jnp.where(top == 0, theirs[1:2], jnp.where(top == 1, theirs[0:1], 0.0))

    margin = dot3(rewards, pairs)
    slope = 1.0 / (1.0 + jnp.exp(margin))
    dreward = -dot3(slope, onehot, NT)
    vrows = []
    for r in range(2):
        half = slice(r * RANK, (r + 1) * RANK)
        dscore = jnp.sum(maskv[...] * dreward[r : r + 1], axis=1, keepdims=True)
        qa[:, half] = (dscore * apre[:, half]).astype(BF16)
        qb[0:ROWS, half] = (dscore * cpre[:, half]).astype(BF16)
        vrows.append(jnp.sum(dscore * vpre[:, half], axis=0, keepdims=True))
    arow2 = lax.broadcasted_iota(I32, (AUG, RANK), 0)
    for r in range(2):
        hi, lo = split(vrows[r])
        tile = jnp.where((arow2 == 3 * r) | (arow2 == 3 * r + 2), hi.astype(F32), 0.0)
        tile = jnp.where(arow2 == 3 * r + 1, lo.astype(F32), tile)
        qb[ROWS : ROWS + AUG, r * RANK : (r + 1) * RANK] = tile.astype(BF16)
    mbd[...] = jnp.where(same, dot(lows[...], qb[0:ROWS, :], TN), 0.0).astype(BF16)

    def feature_chunk(k):
        return lax.rem(zl + OFFSETS[k], NZL)

    def target(u):
        return lax.rem(z + UNITS[u][1] + NZ, NZ)

    def place_of(u):
        half = lax.div(target(u), NZL)
        return UNITS[u][0], jnp.where(half == zh, 0, 1)

    places = [place_of(u) for u in range(len(UNITS))]

    def c1copy(u):
        return remote(gr.at[places[u]], rc.at[places[u]], c1s.at[u], c1r.at[u], core_peer)

    def spread(k, tmp, n, rows):
        for d in range(NY):
            own = tmp[pl.ds(pl.multiple_of((2 * d + c) * n, 16), n), :]
            other = tmp[pl.ds(pl.multiple_of((2 * d + 1 - c) * n, 16), n), :].astype(BF16)
            for r in range(2):
                g32[k, r, d, rows, :] = own[:, r * RANK : (r + 1) * RANK]
                gr[k, r, d, rows, :] = other[:, r * RANK : (r + 1) * RANK]

    def terms(k):
        j = feature_chunk(k)
        for i in range(4):
            cols = pl.ds(pl.multiple_of(j * 1024 + i * 256, 256), 256)
            tmpa[i * 256 : (i + 1) * 256, :] = dot(xa[:, cols], qa[...], TN)
        spread(k, tmpa, RA, slice(0, RA))
        for i in range(3):
            first = j * 1152 + i * 384
            cols = pl.ds(pl.multiple_of(first, 128), 384)
            tmpb[i * 384 : (i + 1) * 384, :] = dot(xb[:, cols], qb[...], TN) + dot(
                wcat(WA + first, 384), mbd[...]
            )
        spread(k, tmpb, RB, slice(RA, RAB))

    ya = y + 1 - 2 * lax.rem(y, 2)
    yb = 3 - y
    cut = (slice(0, RA), slice(RA, RAB))

    def flip(v):
        return v + 1 - 2 * lax.rem(v, 2)

    def sent1(p, i):
        to = (ya, yb)[p]
        return to if i == 0 else ((3 - to) if p == 0 else flip(to))

    def ycopy1(u, p, i):
        return remote(
            b1.at[u, i, pl.ds(*((0, RA), (RA, RB))[p])], (s2a, s2b)[p].at[u, i],
            y1s.at[u, p, i], y1r.at[u, p, i], dev(x, z, (ya, yb)[p] * NC + c),
        )

    def ycopy2(u, p):
        buf = (sa, sb)[p]
        return remote(
            buf.at[0, u], buf.at[1, u], y2s.at[u, p], y2r.at[u, p], dev(x, z, (yb, ya)[p] * NC + c)
        )

    def fcopy(u):
        return remote(b2.at[u], fin.at[z], fs.at[u], fr.at[z], dev(x, target(u), yc))

    def coresum(u, p, chunk):
        k, r = places[u]
        return g32[k, r, chunk, cut[p], :] + rc[k, r, chunk, cut[p], :].astype(F32)

    def step1(u):
        c1copy(u).wait_recv()
        for i in (1, 0):
            for p in range(2):
                b1[u, i, cut[p], :] = coresum(u, p, sent1(p, i)).astype(BF16)
                ycopy1(u, p, i).start()

    def kept(u, p, chunk, i):
        return coresum(u, p, chunk) + (s2a, s2b)[p][u, i].astype(F32)

    def step2(u):
        for p in range(2):
            ycopy1(u, p, 1).wait_recv()
            (sa, sb)[p][0, u] = kept(u, p, (yb, ya)[p], 1).astype(BF16)
            ycopy2(u, p).start()

    def sent(u):
        c1copy(u).wait_send()
        for p in range(2):
            for i in range(2):
                ycopy1(u, p, i).wait_send()
            ycopy2(u, p).wait_send()
        if UNITS[u][1] != 0:
            fcopy(u).wait_send()

    def step3(u):
        for p in range(2):
            ycopy1(u, p, 0).wait_recv()
            ycopy2(u, p).wait_recv()
            total = kept(u, p, y, 0) + (sa, sb)[p][1, u].astype(F32)
            b2[u, cut[p], :] = total.astype(BF16)
        if UNITS[u][1] == 0:
            fin[z] = b2[u]
        else:
            fcopy(u).start()

    terms(0)
    c1copy(0).start()
    for u in range(len(UNITS) + 4):
        if u + 1 < NZL:
            terms(u + 1)
            c1copy(u + 1).start()
        if u + 1 == NZL - 1:
            for later in range(NZL, len(UNITS)):
                c1copy(later).start()
        if u < len(UNITS):
            step1(u)
        if 2 <= u < len(UNITS) + 2:
            step2(u - 2)
        if u >= 4:
            step3(u - 4)
        if u >= 5:
            sent(u - 5)
        if u == len(UNITS) // 2:
            for copy in sends1 + sends2:
                copy.wait_send()
            soft = jnp.log1p(jnp.exp(-jnp.abs(margin))) + jnp.maximum(-margin, 0.0)
            loss = jnp.sum(jnp.where(even8 & (top == 0), soft, 0.0)) * (2.0 / RESP)
    for d in range(1, NZ):
        other = lax.rem(z + d, NZ)
        remote(b2.at[0], fin.at[other], fs.at[0], fr.at[other], dev(x, other, yc)).wait_recv()
    total = fin[0].astype(F32)
    for i in range(1, NZ):
        total = total + fin[i].astype(F32)
    out_ref[0:RAB, :] = total
    out_ref[RAB : RAB + 8, :] = jnp.full((8, RANK), loss, F32)

    sent(len(UNITS) - 1)


def divide(whole, loss, ga, gb):
    ga[0] = whole[0:RA]
    gb[0] = whole[RA:RAB]
    loss[0] = jnp.max(whole[RAB : RAB + 8])


def per_device(acts, base, down_matrices, up_matrices, head, gain, lengths, pairing):
    hbm = pl.BlockSpec(memory_space=pltpu.HBM)
    vmem = pl.BlockSpec(memory_space=pltpu.VMEM)
    smem = pl.BlockSpec(memory_space=pltpu.SMEM)
    dma = pltpu.SemaphoreType.DMA
    whole = pl.pallas_call(
        kernel,
        out_shape=jax.ShapeDtypeStruct((RAB + 8, RANK), F32),
        in_specs=[hbm] * 8,
        out_specs=vmem,
        scratch_shapes=[
            pltpu.VMEM((ROWS, WA), BF16),
            pltpu.VMEM((ROWS + AUG, WB), BF16),
            pltpu.VMEM((2, WAB, RANK), BF16),
            pltpu.VMEM((1, WB), BF16),
            pltpu.VMEM((WB // 128, 128), F32),
            pltpu.SMEM((1, 4), I32),
            pltpu.VMEM((1, RESP), I32),
            pltpu.VMEM((40, 128), F32),
            pltpu.VMEM((40, 128), F32),
            pltpu.VMEM((2 * RANK, 2 * RANK), F32),
            pltpu.VMEM((ROWS, RESP), F32),
            pltpu.VMEM((ROWS, 2 * RANK), F32),
            pltpu.VMEM((ROWS, 2 * RANK), F32),
            pltpu.VMEM((ROWS, 2 * RANK), F32),
            pltpu.VMEM((NY * NC, 8, RESP), F32),
            pltpu.VMEM((NZ, 8, RESP), F32),
            pltpu.VMEM((ROWS, 2 * RANK), BF16),
            pltpu.VMEM((ROWS, 2 * RANK), BF16),
            pltpu.VMEM((ROWS + AUG, 2 * RANK), BF16),
            pltpu.VMEM((2 * RANK, 2 * RANK), BF16),
            pltpu.VMEM((WA // NZL, 2 * RANK), F32),
            pltpu.VMEM((WB // NZL, 2 * RANK), F32),
            pltpu.VMEM((NZL, 2, NY, RAB, RANK), F32),
            pltpu.VMEM((NZL, 2, NY, RAB, RANK), BF16),
            pltpu.VMEM((NZL, 2, NY, RAB, RANK), BF16),
            pltpu.VMEM((2 * NZL, 2, RAB, RANK), BF16),
            pltpu.VMEM((2 * NZL, 2, RA, RANK), BF16),
            pltpu.VMEM((2 * NZL, 2, RB, RANK), BF16),
            pltpu.VMEM((2, 2 * NZL, RA, RANK), BF16),
            pltpu.VMEM((2, 2 * NZL, RB, RANK), BF16),
            pltpu.VMEM((2 * NZL, RAB, RANK), BF16),
            pltpu.VMEM((NZ, RAB, RANK), BF16),
            dma((8,)),
            dma((3, XP)),
            dma((3, XP)),
            dma((WCH,)),
            dma((WCH,)),
            dma((NY, WCH)),
            dma((NY, WCH)),
            dma((NY, WCH)),
            dma((NY, WCH)),
            dma,
            dma,
            dma((NY * NC,)),
            dma((NY * NC,)),
            dma((NZ,)),
            dma((NZ,)),
            dma((2 * NZL,)),
            dma((2 * NZL,)),
            dma((2 * NZL, 2, 2)),
            dma((2 * NZL, 2, 2)),
            dma((2 * NZL, 2)),
            dma((2 * NZL, 2)),
            dma((2 * NZL,)),
            dma((NZ,)),
        ],
        compiler_params=pltpu.CompilerParams(
            collective_id=0, has_side_effects=True, vmem_limit_bytes=60 * 1024 * 1024
        ),
    )(
        acts, base, down_matrices, up_matrices, head,
        gain.reshape(WB // 128, 128), lengths, pairing.reshape(1, RESP),
    )
    return pl.pallas_call(
        divide,
        out_shape=(
            jax.ShapeDtypeStruct((1,), F32),
            jax.ShapeDtypeStruct((1, RA, RANK), F32),
            jax.ShapeDtypeStruct((1, RB, RANK), F32),
        ),
        in_specs=[vmem],
        out_specs=(smem, vmem, vmem),
    )(whole)


def solution(mesh):
    return jax.shard_map(
        per_device,
        mesh=mesh,
        in_specs=(
            P("dp", "member", None, None),
            P("dp", "member", None, None),
            P("member", None, None),
            P("member", None, None),
            P("member", None),
            P(),
            P("dp", None),
            P(),
        ),
        out_specs=(P("member"), P("member", "dp", None), P("member", "dp", None)),
        check_vma=False,
    )
```

```python
import jax
import jax.numpy as jnp
from jax import lax
from jax.experimental import pallas as pl
from jax.experimental.pallas import tpu as pltpu
from jax.sharding import PartitionSpec as P

F32, BF16, I32 = jnp.float32, jnp.bfloat16, jnp.int32
MESH = pl.DeviceIdType.MESH

NX, NZH, NZL, NY, NC = 4, 2, 4, 4, 2
NZ = NZH * NZL
TOK = 48
ROWS = NX * TOK
AUG = 16
WA, WB, RANK = 4096, 4608, 128
RA, RB = 128, 144
RAB = RA + RB
RESP = 128
XA, XB = 3, 3
XP = XA + XB
WAB = WA + WB
WCH = 4
OFFSETS = (0, 3, 1, 2)
UNITS = ((0, 4), (1, 3), (2, -3), (3, 2), (3, -2), (2, 1), (1, -1), (0, 0))
KA, KB = 2048, 2304
TN = (((0,), (0,)), ((), ()))
NT = (((1,), (1,)), ((), ()))


def dot(a, b, dims=(((1,), (0,)), ((), ()))):
    return lax.dot_general(a, b, dims, preferred_element_type=F32)


def split(v):
    hi = v.astype(BF16)
    return hi, (v - hi.astype(F32)).astype(BF16)


def dot3(v, b, dims=(((1,), (0,)), ((), ()))):
    hi = v.astype(BF16)
    rest = v - hi.astype(F32)
    mid = rest.astype(BF16)
    low = (rest - mid.astype(F32)).astype(BF16)
    return dot(hi, b, dims) + dot(mid, b, dims) + dot(low, b, dims)


def kernel(
    acts, base, down, up, head, gain, lengths, pairing,
    out_ref,
    xa, xb, wv, hv, gv, lv, pv, hpk, hrecv, maskv, apre, cpre, vpre, rs1, rs2,
    lows, qa, qb, mbd, tmpa, tmpb, g32, gr, rc, b1a, b1b, s2a, s2b, sa, sb, b2, fin,
    loc, xs, xr, zs, zr, ws, wr, cs, cr, hs, hr, r1s, r1r, r2s, r2r,
    c1s, c1r, y1s, y1r, y2s, y2r, fs, fr,
):
    me_m, me_d = lax.axis_index("member"), lax.axis_index("dp")
    zh, x = lax.div(me_m, NX), lax.rem(me_m, NX)
    zl = lax.div(me_d, NY * NC)
    yc = lax.rem(me_d, NY * NC)
    y, c = lax.div(yc, NC), lax.rem(yc, NC)
    z = zh * NZL + zl

    def dev(x_, z_, yc_):
        return (lax.div(z_, NZL) * NX + x_, lax.rem(z_, NZL) * (NY * NC) + yc_)

    def remote(src, dst, ssem, rsem, to):
        return pltpu.make_async_remote_copy(
            src_ref=src, dst_ref=dst, send_sem=ssem, recv_sem=rsem, device_id=to, device_id_type=MESH
        )

    right, left = lax.rem(x + 1, NX), lax.rem(x + 3, NX)
    zother = lax.rem(z + NZL, NZ)
    core_peer = dev(x, z, y * NC + 1 - c)

    def load(i):
        return pltpu.make_async_copy(*(
            (head, hv), (gain, gv), (lengths, lv), (pairing, pv),
            (acts.at[0, 0], xa.at[pl.ds(0, TOK)]), (base.at[0, 0], xb.at[pl.ds(0, TOK)]),
            (down.at[0], wv.at[0, pl.ds(0, WA)]), (up.at[0], wv.at[0, pl.ds(WA, WB)]),
        )[i], loc.at[i])

    barrier = pltpu.get_barrier_semaphore()
    peers = [dev(right, z, yc), dev(left, z, yc)]
    peers += [dev(x, lax.rem(z + d, NZ), yc) for d in range(1, NZ)]
    peers += [dev(x, z, lax.rem(yc + d, NY * NC)) for d in range(1, NY * NC)]
    for peer in peers:
        pl.semaphore_signal(barrier, inc=1, device_id=peer, device_id_type=MESH)
    for i in (4, 5, 0, 2, 3, 1, 6, 7):
        load(i).start()
    pl.semaphore_wait(barrier, len(peers))

    def xpiece(i, slot):
        if i < XA:
            n = TOK // XA
            return xa.at[pl.ds(slot * TOK + i * n, n)]
        n = TOK // XB
        return xb.at[pl.ds(slot * TOK + (i - XA) * n, n)]

    def xcopy(i, way):
        if way == 0:
            return remote(xpiece(i, 0), xpiece(i, 1), xs.at[0, i], xr.at[0, i], dev(right, z, yc))
        if way == 1:
            return remote(xpiece(i, 0), xpiece(i, 2), xs.at[1, i], xr.at[1, i], dev(left, z, yc))
        turn = c if i < XA else 1 - c
        onward = lax.rem(x + 1 + 2 * turn, NX)
        return remote(xpiece(i, 1 + turn), xpiece(i, 3), xs.at[2, i], xr.at[2, i], dev(onward, z, yc))

    def xwait(i, way):
        xcopy(i, way).wait_recv()

    def xwait_side(i, onward):
        first = 0 if (i < XA) == onward else 1

        @pl.when(c == 0)
        def _():
            xwait(i, first)

        @pl.when(c == 1)
        def _():
            xwait(i, 1 - first)

    def wpiece(i, eighth):
        n = (WA if i < WCH // 2 else WB) // (NY * NC) // (WCH // 2)
        first = eighth * (2 * n) + (i % (WCH // 2)) * n
        return pl.multiple_of(first, 16), n

    def wrows(i, eighth):
        first, n = wpiece(i, eighth)
        return wv.at[1, pl.ds(first + (0 if i < WCH // 2 else WA), n)]

    def zcopy(i):
        src = (down if i < WCH // 2 else up).at[0, pl.ds(*wpiece(i, yc))]
        return remote(src, wrows(i, yc), zs.at[i], zr.at[i], dev(x, zother, yc))

    def wcopy(i, d):
        to = lax.rem(y + d, NY)
        return remote(wrows(i, yc), wrows(i, yc), ws.at[d, i], wr.at[d, i], dev(x, z, to * NC + c))

    def wfrom(d, core):
        return lax.rem(y + NY - d, NY) * NC + core

    def ccopy(i, d, core):
        rows = wrows(i, wfrom(d, core))
        return remote(rows, rows, cs.at[d, i], cr.at[d, i], core_peer)

    load(4).wait()
    load(5).wait()
    for i in range(XP):
        xcopy(i, 0).start()
        xcopy(i, 1).start()
    for i in range(WCH):
        zcopy(i).start()
    load(0).wait()
    for i in range(WB // 128):
        hpk[i : i + 1, :] = hv[0:1, i * 128 : (i + 1) * 128].astype(F32)
    hcopy = remote(hpk, hrecv, hs, hr, dev(x, zother, yc))
    hcopy.start()

    load(2).wait()
    load(3).wait()
    row = lax.broadcasted_iota(I32, (ROWS, RESP), 0)
    slot = jnp.where(row < TOK, 0, jnp.where(row < 2 * TOK, 3, jnp.where(row < 3 * TOK, 1, 2)))
    shift = jnp.where(row < TOK, 0, jnp.where(row < 2 * TOK, 1, jnp.where(row < 3 * TOK, 2, 3)))
    block = x + slot
    block = jnp.where(block >= NX, block - NX, block)
    position = zh * ROWS + block * TOK + row - shift * TOK
    lens = [lv[0, k] for k in range(4)]
    lane = lax.broadcasted_iota(I32, (1, RESP), 1) - me_d * 4
    starts = jnp.zeros((1, RESP), I32)
    ends = jnp.zeros((1, RESP), I32)
    counts = jnp.ones((1, RESP), I32)
    begin = 0
    for k in range(4):
        starts = jnp.where(lane == k, begin, starts)
        begin = begin + lens[k]
        ends = jnp.where(lane == k, begin, ends)
        counts = jnp.where(lane == k, lens[k], counts)
    inverse = 1.0 / counts.astype(F32)
    maskv[...] = jnp.where((position >= starts) & (position < ends), inverse, 0.0)
    order = jnp.broadcast_to(pv[0:1, :], (8, RESP))
    even8 = lax.rem(lax.broadcasted_iota(I32, (8, RESP), 1), 2) == 0
    swapped = jnp.where(even8, pltpu.roll(order, RESP - 1, 1), pltpu.roll(order, 1, 1))
    number = lax.broadcasted_iota(I32, (RESP, RESP), 0)
    sign = jnp.where(lax.rem(lax.broadcasted_iota(I32, (1, RESP), 1), 2) == 0, 1.0, -1.0)
    onehot = jnp.where(number == order[0:1], sign, 0.0)
    pairs = (onehot - jnp.where(number == swapped[0:1], sign, 0.0)).astype(BF16)
    onehot = onehot.astype(BF16)

    def gram_of(r):
        def step(i, g):
            u = wv[r, pl.ds(pl.multiple_of(WA + i * KB, 16), KB), :]
            return g + dot(u, u, TN)

        return split(lax.fori_loop(0, WB // KB, step, jnp.zeros((RANK, RANK), F32)))

    load(6).wait()
    load(7).wait()
    grams = [gram_of(0)]

    for i in range(XP):
        if i < WCH:
            zcopy(i).wait_recv()
            for d in range(1, NY):
                wcopy(i, d).start()
            ccopy(i, 0, c).start()
        xwait_side(i, True)
        xcopy(i, 2).start()

    hcopy.wait_recv()
    load(1).wait()
    arow = lax.broadcasted_iota(I32, (AUG, 128), 0)
    for i in range(WB // 128):
        cols = slice(i * 128, (i + 1) * 128)
        g = gv[i : i + 1, :]
        hi0, lo0 = split(hpk[i : i + 1, :] * g)
        hi1, lo1 = split(hrecv[i : i + 1, :] * g)
        tile = jnp.where(arow < 2, hi0.astype(F32), 0.0)
        tile = jnp.where(arow == 2, lo0.astype(F32), tile)
        tile = jnp.where((arow == 3) | (arow == 4), hi1.astype(F32), tile)
        tile = jnp.where(arow == 5, lo1.astype(F32), tile)
        xb[ROWS : ROWS + AUG, cols] = tile.astype(BF16)

    def share(pieces):
        for i in pieces:
            for d in range(1, NY):
                remote(
                    wrows(i, wfrom(d, c)), wrows(i, wfrom(d, c)), ws.at[d, i], wr.at[d, i], core_peer
                ).wait_recv()
                ccopy(i, d, c).start()

    def shared(pieces):
        for i in pieces:
            for d in range(NY):
                ccopy(i, d, 1 - c).wait_recv()

    def wcat(first, n):
        rows = pl.ds(pl.multiple_of(first, 16), n)
        return jnp.concatenate([wv[0, rows, :], wv[1, rows, :]], axis=1)

    def forward_a(first, n, begin, end, acc):
        rows = pl.ds(first, n)

        def step(i, acc):
            k = pl.ds(pl.multiple_of(i * KA, KA), KA)
            return acc + dot(xa[rows, k], wcat(i * KA, KA))

        return lax.fori_loop(begin, end, step, acc)

    def nothing(n):
        return jnp.zeros((n, 2 * RANK), F32), (
            jnp.zeros((n, 2 * RANK), F32), jnp.zeros((n, AUG), F32), jnp.zeros((n, 128), F32),
        )

    share(range(WCH // 2))
    shared(range(WCH // 2))
    for i in range(XA):
        xwait_side(i, False)
    near_a, near_b = nothing(3 * TOK)
    near_a = forward_a(0, 3 * TOK, 0, WA // KA, near_a)
    share(range(WCH // 2, WCH))
    for i in range(XA, XP):
        xwait_side(i, False)

    top = lax.broadcasted_iota(I32, (8, RESP), 0)

    def heads(block, k, acc):
        bh, nb = acc
        wide = block.astype(F32)
        square = wide * wide
        for j in range(KB // 128):
            nb = nb + square[:, j * 128 : (j + 1) * 128]
        return bh + dot(block, xb[pl.ds(ROWS, AUG), k], NT), nb

    def near_heads(i, acc):
        k = pl.ds(pl.multiple_of(i * KB, KB), KB)
        return heads(xb[0 : 3 * TOK, k], k, acc)

    def near_b_step(i, acc):
        t, h = acc
        k = pl.ds(pl.multiple_of(i * KB, KB), KB)
        u = wcat(WA + i * KB, KB)
        return t + dot(xb[0 : 3 * TOK, k], u), h + dot(xb[pl.ds(ROWS, AUG), k], u)

    def far_b_step(i, acc):
        t, *rest = acc
        k = pl.ds(pl.multiple_of(i * KB, KB), KB)
        block = xb[pl.ds(3 * TOK, TOK), k]
        return t + dot(block, wcat(WA + i * KB, KB)), *heads(block, k, rest)

    t, *near_sums = near_b
    near_sums = lax.fori_loop(0, WB // KB, near_heads, tuple(near_sums))
    shared(range(WCH // 2, WCH))
    t, uh16 = lax.fori_loop(0, WB // KB, near_b_step, (t, jnp.zeros((AUG, 2 * RANK), F32)))
    grams.append(gram_of(1))
    lane2 = lax.broadcasted_iota(I32, (1, 2 * RANK), 1)
    uh = jnp.where(lane2 < RANK, uh16[0:1] + uh16[2:3], uh16[3:4] + uh16[5:6])
    same = (lax.broadcasted_iota(I32, (2 * RANK, 2 * RANK), 0) < RANK) == (
        lax.broadcasted_iota(I32, (2 * RANK, 2 * RANK), 1) < RANK
    )

    def early(low32, rows):
        low = low32.astype(BF16)
        lowf = low.astype(F32)
        lows[rows, :] = low
        along = lowf * uh
        lowg, sums = [], []
        for r, (hi, lo) in enumerate(grams):
            half = slice(r * RANK, (r + 1) * RANK)
            lowg.append(dot(low[:, half], hi) + dot(low[:, half], lo))
            sums.append(jnp.sum(along[:, half], axis=1, keepdims=True))
        return lowf, jnp.concatenate(lowg, axis=1), sums

    def scores(rows, before, acc):
        lowf, lowg, along = before
        t, bh, nb = acc
        yu = t + lowg
        cross = lowf * (t + yu)
        norm = jnp.sum(nb, axis=1, keepdims=True)
        rewards = []
        for r in range(2):
            half = slice(r * RANK, (r + 1) * RANK)
            n2 = jnp.maximum(norm + jnp.sum(cross[:, half], axis=1, keepdims=True), 0.0)
            s = lax.rsqrt(n2 * (1.0 / WB) + 1e-06)
            yh = (
                bh[:, 3 * r : 3 * r + 1]
                + bh[:, 3 * r + 2 : 3 * r + 3]
                + along[r]
            )
            cc = s * s * s * (yh * (1.0 / WB))
            apre[rows, half] = s * uh[:, half] - cc * yu[:, half]
            cpre[rows, half] = -cc * lowf[:, half]
            vpre[rows, half] = s * lowf[:, half]
            rewards.append(jnp.sum(maskv[rows, :] * (s * yh), axis=0, keepdims=True))
        return jnp.where(top == 0, rewards[0], jnp.where(top == 1, rewards[1], 0.0))

    near = pl.ds(0, 3 * TOK)
    tile = scores(near, early(near_a, near), (t, *near_sums))
    far_a, far_b = nothing(TOK)
    for i in range(XA):
        xwait(i, 2)
    far_a = forward_a(3 * TOK, TOK, 0, WA // KA, far_a)
    far = pl.ds(3 * TOK, TOK)
    before = early(far_a, far)
    for i in range(XB):
        xwait(XA + i, 2)
    far_b = lax.fori_loop(0, WB // KB, far_b_step, far_b)
    tile = tile + scores(far, before, far_b)

    rs1[yc] = tile
    sends1 = []
    for d in range(1, NY * NC):
        other = lax.rem(yc + d, NY * NC)
        copy = remote(rs1.at[yc], rs1.at[yc], r1s.at[d], r1r.at[yc], dev(x, z, other))
        copy.start()
        sends1.append(copy)
    hcopy.wait_send()
    for i in range(XP):
        for way in range(3):
            xcopy(i, way).wait_send()

    for i in range(WCH):
        zcopy(i).wait_send()
        for d in range(NY):
            ccopy(i, d, c).wait_send()
            if d:
                wcopy(i, d).wait_send()
    for d in range(1, NY * NC):
        other = lax.rem(yc + d, NY * NC)
        remote(rs1.at[other], rs1.at[other], r1s.at[d], r1r.at[other], dev(x, z, other)).wait_recv()
    rs2[z] = jnp.sum(rs1[...], axis=0)
    sends2 = []
    for d in range(1, NZ):
        other = lax.rem(z + d, NZ)
        copy = remote(rs2.at[z], rs2.at[z], r2s.at[d], r2r.at[z], dev(x, other, yc))
        copy.start()
        sends2.append(copy)
    for d in range(1, NZ):
        other = lax.rem(z + d, NZ)
        remote(rs2.at[other], rs2.at[other], r2s.at[d], r2r.at[other], dev(x, other, yc)).wait_recv()
    mine = jnp.sum(rs2[pl.ds(zh * NZL, NZL)], axis=0)
    theirs = jnp.sum(rs2[pl.ds((1 - zh) * NZL, NZL)], axis=0)
    rewards = mine + jnp.where(top == 0, theirs[1:2], jnp.where(top == 1, theirs[0:1], 0.0))

    margin = dot3(rewards, pairs)
    slope = 1.0 / (1.0 + jnp.exp(margin))
    dreward = -dot3(slope, onehot, NT)
    vrows = []
    for r in range(2):
        half = slice(r * RANK, (r + 1) * RANK)
        dscore = jnp.sum(maskv[...] * dreward[r : r + 1], axis=1, keepdims=True)
        qa[:, half] = (dscore * apre[:, half]).astype(BF16)
        qb[0:ROWS, half] = (dscore * cpre[:, half]).astype(BF16)
        vrows.append(jnp.sum(dscore * vpre[:, half], axis=0, keepdims=True))
    arow2 = lax.broadcasted_iota(I32, (AUG, RANK), 0)
    for r in range(2):
        hi, lo = split(vrows[r])
        tile = jnp.where((arow2 == 3 * r) | (arow2 == 3 * r + 2), hi.astype(F32), 0.0)
        tile = jnp.where(arow2 == 3 * r + 1, lo.astype(F32), tile)
        qb[ROWS : ROWS + AUG, r * RANK : (r + 1) * RANK] = tile.astype(BF16)
    mbd[...] = jnp.where(same, dot(lows[...], qb[0:ROWS, :], TN), 0.0).astype(BF16)

    def feature_chunk(k):
        return lax.rem(zl + OFFSETS[k], NZL)

    def target(u):
        return lax.rem(z + UNITS[u][1] + NZ, NZ)

    def place_of(u):
        half = lax.div(target(u), NZL)
        return UNITS[u][0], jnp.where(half == zh, 0, 1)

    places = [place_of(u) for u in range(len(UNITS))]

    def c1copy(u):
        return remote(gr.at[places[u]], rc.at[places[u]], c1s.at[u], c1r.at[u], core_peer)

    def spread(k, tmp, n, rows):
        for d in range(NY):
            own = tmp[pl.ds(pl.multiple_of((2 * d + c) * n, 16), n), :]
            other = tmp[pl.ds(pl.multiple_of((2 * d + 1 - c) * n, 16), n), :].astype(BF16)
            for r in range(2):
                g32[k, r, d, rows, :] = own[:, r * RANK : (r + 1) * RANK]
                gr[k, r, d, rows, :] = other[:, r * RANK : (r + 1) * RANK]

    def terms(k):
        j = feature_chunk(k)
        for i in range(4):
            cols = pl.ds(pl.multiple_of(j * 1024 + i * 256, 256), 256)
            tmpa[i * 256 : (i + 1) * 256, :] = dot(xa[:, cols], qa[...], TN)
        spread(k, tmpa, RA, slice(0, RA))
        for i in range(3):
            first = j * 1152 + i * 384
            cols = pl.ds(pl.multiple_of(first, 128), 384)
            tmpb[i * 384 : (i + 1) * 384, :] = dot(xb[:, cols], qb[...], TN) + dot(
                wcat(WA + first, 384), mbd[...]
            )
        spread(k, tmpb, RB, slice(RA, RAB))

    ya = y + 1 - 2 * lax.rem(y, 2)
    yb = 3 - y
    cut = (slice(0, RA), slice(RA, RAB))

    def flip(v):
        return v + 1 - 2 * lax.rem(v, 2)

    def sent1(p, i):
        to = (ya, yb)[p]
        return to if i == 0 else ((3 - to) if p == 0 else flip(to))

    def ycopy1(u, p):
        return remote(
            (b1a, b1b)[p].at[u], (s2a, s2b)[p].at[u],
            y1s.at[u, p], y1r.at[u, p], dev(x, z, (ya, yb)[p] * NC + c),
        )

    def ycopy2(u, p):
        buf = (sa, sb)[p]
        return remote(
            buf.at[0, u], buf.at[1, u], y2s.at[u, p], y2r.at[u, p], dev(x, z, (yb, ya)[p] * NC + c)
        )

    def fcopy(u):
        return remote(b2.at[u], fin.at[z], fs.at[u], fr.at[z], dev(x, target(u), yc))

    def coresum(u, p, chunk):
        k, r = places[u]
        return g32[k, r, chunk, cut[p], :] + rc[k, r, chunk, cut[p], :].astype(F32)

    def step1(u):
        c1copy(u).wait_recv()
        for p in range(2):
            for i in range(2):
                (b1a, b1b)[p][u, i] = coresum(u, p, sent1(p, i)).astype(BF16)
            ycopy1(u, p).start()

    def kept(u, p, chunk, i):
        return coresum(u, p, chunk) + (s2a, s2b)[p][u, i].astype(F32)

    def step2(u):
        for p in range(2):
            ycopy1(u, p).wait_recv()
            (sa, sb)[p][0, u] = kept(u, p, (yb, ya)[p], 1).astype(BF16)
            ycopy2(u, p).start()

    def sent(u):
        c1copy(u).wait_send()
        for p in range(2):
            ycopy1(u, p).wait_send()
            ycopy2(u, p).wait_send()
        if UNITS[u][1] != 0:
            fcopy(u).wait_send()

    def step3(u):
        for p in range(2):
            ycopy2(u, p).wait_recv()
            total = kept(u, p, y, 0) + (sa, sb)[p][1, u].astype(F32)
            b2[u, cut[p], :] = total.astype(BF16)
        if UNITS[u][1] == 0:
            fin[z] = b2[u]
        else:
            fcopy(u).start()

    terms(0)
    c1copy(0).start()
    for u in range(len(UNITS) + 4):
        if u + 1 < NZL:
            terms(u + 1)
            c1copy(u + 1).start()
        if u + 1 == NZL - 1:
            for later in range(NZL, len(UNITS)):
                c1copy(later).start()
        if u < len(UNITS):
            step1(u)
        if 2 <= u < len(UNITS) + 2:
            step2(u - 2)
        if u >= 4:
            step3(u - 4)
        if u >= 5:
            sent(u - 5)
        if u == len(UNITS) // 2:
            for copy in sends1 + sends2:
                copy.wait_send()
            soft = jnp.log1p(jnp.exp(-jnp.abs(margin))) + jnp.maximum(-margin, 0.0)
            loss = jnp.sum(jnp.where(even8 & (top == 0), soft, 0.0)) * (2.0 / RESP)
    for d in range(1, NZ):
        other = lax.rem(z + d, NZ)
        remote(b2.at[0], fin.at[other], fs.at[0], fr.at[other], dev(x, other, yc)).wait_recv()
    total = fin[0].astype(F32)
    for i in range(1, NZ):
        total = total + fin[i].astype(F32)
    out_ref[0:RAB, :] = total
    out_ref[RAB : RAB + 8, :] = jnp.full((8, RANK), loss, F32)

    sent(len(UNITS) - 1)


def divide(whole, loss, ga, gb):
    ga[0] = whole[0:RA]
    gb[0] = whole[RA:RAB]
    loss[0] = jnp.max(whole[RAB : RAB + 8])


def per_device(acts, base, down_matrices, up_matrices, head, gain, lengths, pairing):
    hbm = pl.BlockSpec(memory_space=pltpu.HBM)
    vmem = pl.BlockSpec(memory_space=pltpu.VMEM)
    smem = pl.BlockSpec(memory_space=pltpu.SMEM)
    dma = pltpu.SemaphoreType.DMA
    whole = pl.pallas_call(
        kernel,
        out_shape=jax.ShapeDtypeStruct((RAB + 8, RANK), F32),
        in_specs=[hbm] * 8,
        out_specs=vmem,
        scratch_shapes=[
            pltpu.VMEM((ROWS, WA), BF16),
            pltpu.VMEM((ROWS + AUG, WB), BF16),
            pltpu.VMEM((2, WAB, RANK), BF16),
            pltpu.VMEM((1, WB), BF16),
            pltpu.VMEM((WB // 128, 128), F32),
            pltpu.SMEM((1, 4), I32),
            pltpu.VMEM((1, RESP), I32),
            pltpu.VMEM((40, 128), F32),
            pltpu.VMEM((40, 128), F32),
            pltpu.VMEM((ROWS, RESP), F32),
            pltpu.VMEM((ROWS, 2 * RANK), F32),
            pltpu.VMEM((ROWS, 2 * RANK), F32),
            pltpu.VMEM((ROWS, 2 * RANK), F32),
            pltpu.VMEM((NY * NC, 8, RESP), F32),
            pltpu.VMEM((NZ, 8, RESP), F32),
            pltpu.VMEM((ROWS, 2 * RANK), BF16),
            pltpu.VMEM((ROWS, 2 * RANK), BF16),
            pltpu.VMEM((ROWS + AUG, 2 * RANK), BF16),
            pltpu.VMEM((2 * RANK, 2 * RANK), BF16),
            pltpu.VMEM((WA // NZL, 2 * RANK), F32),
            pltpu.VMEM((WB // NZL, 2 * RANK), F32),
            pltpu.VMEM((NZL, 2, NY, RAB, RANK), F32),
            pltpu.VMEM((NZL, 2, NY, RAB, RANK), BF16),
            pltpu.VMEM((NZL, 2, NY, RAB, RANK), BF16),
            pltpu.VMEM((2 * NZL, 2, RA, RANK), BF16),
            pltpu.VMEM((2 * NZL, 2, RB, RANK), BF16),
            pltpu.VMEM((2 * NZL, 2, RA, RANK), BF16),
            pltpu.VMEM((2 * NZL, 2, RB, RANK), BF16),
            pltpu.VMEM((2, 2 * NZL, RA, RANK), BF16),
            pltpu.VMEM((2, 2 * NZL, RB, RANK), BF16),
            pltpu.VMEM((2 * NZL, RAB, RANK), BF16),
            pltpu.VMEM((NZ, RAB, RANK), BF16),
            dma((8,)),
            dma((3, XP)),
            dma((3, XP)),
            dma((WCH,)),
            dma((WCH,)),
            dma((NY, WCH)),
            dma((NY, WCH)),
            dma((NY, WCH)),
            dma((NY, WCH)),
            dma,
            dma,
            dma((NY * NC,)),
            dma((NY * NC,)),
            dma((NZ,)),
            dma((NZ,)),
            dma((2 * NZL,)),
            dma((2 * NZL,)),
            dma((2 * NZL, 2)),
            dma((2 * NZL, 2)),
            dma((2 * NZL, 2)),
            dma((2 * NZL, 2)),
            dma((2 * NZL,)),
            dma((NZ,)),
        ],
        compiler_params=pltpu.CompilerParams(
            collective_id=0, has_side_effects=True, vmem_limit_bytes=60 * 1024 * 1024
        ),
    )(
        acts, base, down_matrices, up_matrices, head,
        gain.reshape(WB // 128, 128), lengths, pairing.reshape(1, RESP),
    )
    return pl.pallas_call(
        divide,
        out_shape=(
            jax.ShapeDtypeStruct((1,), F32),
            jax.ShapeDtypeStruct((1, RA, RANK), F32),
            jax.ShapeDtypeStruct((1, RB, RANK), F32),
        ),
        in_specs=[vmem],
        out_specs=(smem, vmem, vmem),
    )(whole)


def solution(mesh):
    return jax.shard_map(
        per_device,
        mesh=mesh,
        in_specs=(
            P("dp", "member", None, None),
            P("dp", "member", None, None),
            P("member", None, None),
            P("member", None, None),
            P("member", None),
            P(),
            P("dp", None),
            P(),
        ),
        out_specs=(P("member"), P("member", "dp", None), P("member", "dp", None)),
        check_vma=False,
    )
```

```python
import jax
import jax.numpy as jnp
from jax import lax
from jax.experimental import pallas as pl
from jax.experimental.pallas import tpu as pltpu
from jax.sharding import PartitionSpec as P

F32, BF16, I32 = jnp.float32, jnp.bfloat16, jnp.int32
MESH = pl.DeviceIdType.MESH

NX, NZH, NZL, NY, NC = 4, 2, 4, 4, 2
NZ = NZH * NZL
TOK = 48
ROWS = NX * TOK
AUG = 16
WA, WB, RANK = 4096, 4608, 128
RA, RB = 128, 144
RAB = RA + RB
RESP = 128
XA, XB = 3, 3
XP = XA + XB
WAB = WA + WB
WCH = 4
OFFSETS = (0, 3, 1, 2)
UNITS = ((0, 4), (1, 3), (2, -3), (3, 2), (3, -2), (2, 1), (1, -1), (0, 0))
KA, KB = 4096, 4608
TN = (((0,), (0,)), ((), ()))
NT = (((1,), (1,)), ((), ()))


def dot(a, b, dims=(((1,), (0,)), ((), ()))):
    return lax.dot_general(a, b, dims, preferred_element_type=F32)


def split(v):
    hi = v.astype(BF16)
    return hi, (v - hi.astype(F32)).astype(BF16)


def dot3(v, b, dims=(((1,), (0,)), ((), ()))):
    hi = v.astype(BF16)
    rest = v - hi.astype(F32)
    mid = rest.astype(BF16)
    low = (rest - mid.astype(F32)).astype(BF16)
    return dot(hi, b, dims) + dot(mid, b, dims) + dot(low, b, dims)


def kernel(
    acts, base, down, up, head, gain, lengths, pairing,
    out_ref,
    xa, xb, wv, hv, gv, lv, pv, hpk, hrecv, maskv, apre, cpre, vpre, rs1, rs2,
    lows, qa, qb, mbd, tmpa, tmpb, g32, gr, rc, b1a, b1b, s2a, s2b, sa, sb, b2, fin,
    loc, xs, xr, zs, zr, ws, wr, cs, cr, hs, hr, r1s, r1r, r2s, r2r,
    c1s, c1r, y1s, y1r, y2s, y2r, fs, fr,
):
    me_m, me_d = lax.axis_index("member"), lax.axis_index("dp")
    zh, x = lax.div(me_m, NX), lax.rem(me_m, NX)
    zl = lax.div(me_d, NY * NC)
    yc = lax.rem(me_d, NY * NC)
    y, c = lax.div(yc, NC), lax.rem(yc, NC)
    z = zh * NZL + zl

    def dev(x_, z_, yc_):
        return (lax.div(z_, NZL) * NX + x_, lax.rem(z_, NZL) * (NY * NC) + yc_)

    def remote(src, dst, ssem, rsem, to):
        return pltpu.make_async_remote_copy(
            src_ref=src, dst_ref=dst, send_sem=ssem, recv_sem=rsem, device_id=to, device_id_type=MESH
        )

    right, left = lax.rem(x + 1, NX), lax.rem(x + 3, NX)
    zother = lax.rem(z + NZL, NZ)
    core_peer = dev(x, z, y * NC + 1 - c)

    def load(i):
        return pltpu.make_async_copy(*(
            (head, hv), (gain, gv), (lengths, lv), (pairing, pv),
            (acts.at[0, 0], xa.at[pl.ds(0, TOK)]), (base.at[0, 0], xb.at[pl.ds(0, TOK)]),
            (down.at[0], wv.at[0, pl.ds(0, WA)]), (up.at[0], wv.at[0, pl.ds(WA, WB)]),
        )[i], loc.at[i])

    barrier = pltpu.get_barrier_semaphore()
    peers = [dev(right, z, yc), dev(left, z, yc)]
    peers += [dev(x, lax.rem(z + d, NZ), yc) for d in range(1, NZ)]
    peers += [dev(x, z, lax.rem(yc + d, NY * NC)) for d in range(1, NY * NC)]
    for peer in peers:
        pl.semaphore_signal(barrier, inc=1, device_id=peer, device_id_type=MESH)
    for i in (4, 5, 0, 2, 3, 1, 6, 7):
        load(i).start()
    pl.semaphore_wait(barrier, len(peers))

    def xpiece(i, slot):
        if i < XA:
            n = TOK // XA
            return xa.at[pl.ds(slot * TOK + i * n, n)]
        n = TOK // XB
        return xb.at[pl.ds(slot * TOK + (i - XA) * n, n)]

    def xcopy(i, way):
        if way == 0:
            return remote(xpiece(i, 0), xpiece(i, 1), xs.at[0, i], xr.at[0, i], dev(right, z, yc))
        if way == 1:
            return remote(xpiece(i, 0), xpiece(i, 2), xs.at[1, i], xr.at[1, i], dev(left, z, yc))
        turn = c if i < XA else 1 - c
        onward = lax.rem(x + 1 + 2 * turn, NX)
        return remote(xpiece(i, 1 + turn), xpiece(i, 3), xs.at[2, i], xr.at[2, i], dev(onward, z, yc))

    def xwait(i, way):
        xcopy(i, way).wait_recv()

    def xwait_side(i, onward):
        first = 0 if (i < XA) == onward else 1

        @pl.when(c == 0)
        def _():
            xwait(i, first)

        @pl.when(c == 1)
        def _():
            xwait(i, 1 - first)

    def wpiece(i, eighth):
        n = (WA if i < WCH // 2 else WB) // (NY * NC) // (WCH // 2)
        first = eighth * (2 * n) + (i % (WCH // 2)) * n
        return pl.multiple_of(first, 16), n

    def wrows(i, eighth):
        first, n = wpiece(i, eighth)
        return wv.at[1, pl.ds(first + (0 if i < WCH // 2 else WA), n)]

    def zcopy(i):
        src = (down if i < WCH // 2 else up).at[0, pl.ds(*wpiece(i, yc))]
        return remote(src, wrows(i, yc), zs.at[i], zr.at[i], dev(x, zother, yc))

    def wcopy(i, d):
        to = lax.rem(y + d, NY)
        return remote(wrows(i, yc), wrows(i, yc), ws.at[d, i], wr.at[d, i], dev(x, z, to * NC + c))

    def wfrom(d, core):
        return lax.rem(y + NY - d, NY) * NC + core

    def ccopy(i, d, core):
        rows = wrows(i, wfrom(d, core))
        return remote(rows, rows, cs.at[d, i], cr.at[d, i], core_peer)

    load(4).wait()
    load(5).wait()
    for i in range(XP):
        xcopy(i, 0).start()
        xcopy(i, 1).start()
    for i in range(WCH):
        zcopy(i).start()
    load(0).wait()
    for i in range(WB // 128):
        hpk[i : i + 1, :] = hv[0:1, i * 128 : (i + 1) * 128].astype(F32)
    hcopy = remote(hpk, hrecv, hs, hr, dev(x, zother, yc))
    hcopy.start()

    load(2).wait()
    load(3).wait()
    row = lax.broadcasted_iota(I32, (ROWS, RESP), 0)
    slot = jnp.where(row < TOK, 0, jnp.where(row < 2 * TOK, 3, jnp.where(row < 3 * TOK, 1, 2)))
    shift = jnp.where(row < TOK, 0, jnp.where(row < 2 * TOK, 1, jnp.where(row < 3 * TOK, 2, 3)))
    block = x + slot
    block = jnp.where(block >= NX, block - NX, block)
    position = zh * ROWS + block * TOK + row - shift * TOK
    lens = [lv[0, k] for k in range(4)]
    lane = lax.broadcasted_iota(I32, (1, RESP), 1) - me_d * 4
    starts = jnp.zeros((1, RESP), I32)
    ends = jnp.zeros((1, RESP), I32)
    counts = jnp.ones((1, RESP), I32)
    begin = 0
    for k in range(4):
        starts = jnp.where(lane == k, begin, starts)
        begin = begin + lens[k]
        ends = jnp.where(lane == k, begin, ends)
        counts = jnp.where(lane == k, lens[k], counts)
    inverse = 1.0 / counts.astype(F32)
    maskv[...] = jnp.where((position >= starts) & (position < ends), inverse, 0.0)
    order = jnp.broadcast_to(pv[0:1, :], (8, RESP))
    even8 = lax.rem(lax.broadcasted_iota(I32, (8, RESP), 1), 2) == 0
    swapped = jnp.where(even8, pltpu.roll(order, RESP - 1, 1), pltpu.roll(order, 1, 1))
    number = lax.broadcasted_iota(I32, (RESP, RESP), 0)
    sign = jnp.where(lax.rem(lax.broadcasted_iota(I32, (1, RESP), 1), 2) == 0, 1.0, -1.0)
    onehot = jnp.where(number == order[0:1], sign, 0.0)
    pairs = (onehot - jnp.where(number == swapped[0:1], sign, 0.0)).astype(BF16)
    onehot = onehot.astype(BF16)

    def gram_of(r):
        def step(i, g):
            u = wv[r, pl.ds(pl.multiple_of(WA + i * KB, 16), KB), :]
            return g + dot(u, u, TN)

        return split(lax.fori_loop(0, WB // KB, step, jnp.zeros((RANK, RANK), F32)))

    load(6).wait()
    load(7).wait()
    grams = [gram_of(0)]

    for i in range(XP):
        if i < WCH:
            zcopy(i).wait_recv()
            for d in range(1, NY):
                wcopy(i, d).start()
            ccopy(i, 0, c).start()
        xwait_side(i, True)
        xcopy(i, 2).start()

    hcopy.wait_recv()
    load(1).wait()
    arow = lax.broadcasted_iota(I32, (AUG, 128), 0)
    for i in range(WB // 128):
        cols = slice(i * 128, (i + 1) * 128)
        g = gv[i : i + 1, :]
        hi0, lo0 = split(hpk[i : i + 1, :] * g)
        hi1, lo1 = split(hrecv[i : i + 1, :] * g)
        tile = jnp.where(arow < 2, hi0.astype(F32), 0.0)
        tile = jnp.where(arow == 2, lo0.astype(F32), tile)
        tile = jnp.where((arow == 3) | (arow == 4), hi1.astype(F32), tile)
        tile = jnp.where(arow == 5, lo1.astype(F32), tile)
        xb[ROWS : ROWS + AUG, cols] = tile.astype(BF16)

    def share(pieces):
        for i in pieces:
            for d in range(1, NY):
                remote(
                    wrows(i, wfrom(d, c)), wrows(i, wfrom(d, c)), ws.at[d, i], wr.at[d, i], core_peer
                ).wait_recv()
                ccopy(i, d, c).start()

    def shared(pieces):
        for i in pieces:
            for d in range(NY):
                ccopy(i, d, 1 - c).wait_recv()

    def wcat(first, n):
        rows = pl.ds(pl.multiple_of(first, 16), n)
        return jnp.concatenate([wv[0, rows, :], wv[1, rows, :]], axis=1)

    def forward_a(first, n, begin, end, acc):
        rows = pl.ds(first, n)

        def step(i, acc):
            k = pl.ds(pl.multiple_of(i * KA, KA), KA)
            return acc + dot(xa[rows, k], wcat(i * KA, KA))

        return lax.fori_loop(begin, end, step, acc)

    def nothing(n):
        return jnp.zeros((n, 2 * RANK), F32), (
            jnp.zeros((n, 2 * RANK), F32), jnp.zeros((n, AUG), F32), jnp.zeros((n, 128), F32),
        )

    share(range(WCH // 2))
    shared(range(WCH // 2))
    for i in range(XA):
        xwait_side(i, False)
    near_a, near_b = nothing(3 * TOK)
    near_a = forward_a(0, 3 * TOK, 0, WA // KA, near_a)
    share(range(WCH // 2, WCH))
    for i in range(XA, XP):
        xwait_side(i, False)

    top = lax.broadcasted_iota(I32, (8, RESP), 0)

    def heads(block, k, acc):
        bh, nb = acc
        wide = block.astype(F32)
        square = wide * wide
        for j in range(KB // 128):
            nb = nb + square[:, j * 128 : (j + 1) * 128]
        return bh + dot(block, xb[pl.ds(ROWS, AUG), k], NT), nb

    def near_heads(i, acc):
        k = pl.ds(pl.multiple_of(i * KB, KB), KB)
        return heads(xb[0 : 3 * TOK, k], k, acc)

    def near_b_step(i, acc):
        t, h = acc
        k = pl.ds(pl.multiple_of(i * KB, KB), KB)
        u = wcat(WA + i * KB, KB)
        return t + dot(xb[0 : 3 * TOK, k], u), h + dot(xb[pl.ds(ROWS, AUG), k], u)

    def far_b_step(i, acc):
        t, *rest = acc
        k = pl.ds(pl.multiple_of(i * KB, KB), KB)
        block = xb[pl.ds(3 * TOK, TOK), k]
        return t + dot(block, wcat(WA + i * KB, KB)), *heads(block, k, rest)

    t, *near_sums = near_b
    near_sums = lax.fori_loop(0, WB // KB, near_heads, tuple(near_sums))
    shared(range(WCH // 2, WCH))
    t, uh16 = lax.fori_loop(0, WB // KB, near_b_step, (t, jnp.zeros((AUG, 2 * RANK), F32)))
    grams.append(gram_of(1))
    lane2 = lax.broadcasted_iota(I32, (1, 2 * RANK), 1)
    uh = jnp.where(lane2 < RANK, uh16[0:1] + uh16[2:3], uh16[3:4] + uh16[5:6])
    same = (lax.broadcasted_iota(I32, (2 * RANK, 2 * RANK), 0) < RANK) == (
        lax.broadcasted_iota(I32, (2 * RANK, 2 * RANK), 1) < RANK
    )

    def early(low32, rows):
        low = low32.astype(BF16)
        lowf = low.astype(F32)
        lows[rows, :] = low
        along = lowf * uh
        lowg, sums = [], []
        for r, (hi, lo) in enumerate(grams):
            half = slice(r * RANK, (r + 1) * RANK)
            lowg.append(dot(low[:, half], hi) + dot(low[:, half], lo))
            sums.append(jnp.sum(along[:, half], axis=1, keepdims=True))
        return lowf, jnp.concatenate(lowg, axis=1), sums

    def scores(rows, before, acc):
        lowf, lowg, along = before
        t, bh, nb = acc
        yu = t + lowg
        cross = lowf * (t + yu)
        norm = jnp.sum(nb, axis=1, keepdims=True)
        rewards = []
        for r in range(2):
            half = slice(r * RANK, (r + 1) * RANK)
            n2 = jnp.maximum(norm + jnp.sum(cross[:, half], axis=1, keepdims=True), 0.0)
            s = lax.rsqrt(n2 * (1.0 / WB) + 1e-06)
            yh = (
                bh[:, 3 * r : 3 * r + 1]
                + bh[:, 3 * r + 2 : 3 * r + 3]
                + along[r]
            )
            cc = s * s * s * (yh * (1.0 / WB))
            apre[rows, half] = s * uh[:, half] - cc * yu[:, half]
            cpre[rows, half] = -cc * lowf[:, half]
            vpre[rows, half] = s * lowf[:, half]
            rewards.append(jnp.sum(maskv[rows, :] * (s * yh), axis=0, keepdims=True))
        return jnp.where(top == 0, rewards[0], jnp.where(top == 1, rewards[1], 0.0))

    near = pl.ds(0, 3 * TOK)
    tile = scores(near, early(near_a, near), (t, *near_sums))
    far_a, far_b = nothing(TOK)
    for i in range(XA):
        xwait(i, 2)
    far_a = forward_a(3 * TOK, TOK, 0, WA // KA, far_a)
    far = pl.ds(3 * TOK, TOK)
    before = early(far_a, far)
    for i in range(XB):
        xwait(XA + i, 2)
    far_b = lax.fori_loop(0, WB // KB, far_b_step, far_b)
    tile = tile + scores(far, before, far_b)

    rs1[yc] = tile
    sends1 = []
    for d in range(1, NY * NC):
        other = lax.rem(yc + d, NY * NC)
        copy = remote(rs1.at[yc], rs1.at[yc], r1s.at[d], r1r.at[yc], dev(x, z, other))
        copy.start()
        sends1.append(copy)
    hcopy.wait_send()
    for i in range(XP):
        for way in range(3):
            xcopy(i, way).wait_send()

    for i in range(WCH):
        zcopy(i).wait_send()
        for d in range(NY):
            ccopy(i, d, c).wait_send()
            if d:
                wcopy(i, d).wait_send()
    for d in range(1, NY * NC):
        other = lax.rem(yc + d, NY * NC)
        remote(rs1.at[other], rs1.at[other], r1s.at[d], r1r.at[other], dev(x, z, other)).wait_recv()
    rs2[z] = jnp.sum(rs1[...], axis=0)
    sends2 = []
    for d in range(1, NZ):
        other = lax.rem(z + d, NZ)
        copy = remote(rs2.at[z], rs2.at[z], r2s.at[d], r2r.at[z], dev(x, other, yc))
        copy.start()
        sends2.append(copy)
    for d in range(1, NZ):
        other = lax.rem(z + d, NZ)
        remote(rs2.at[other], rs2.at[other], r2s.at[d], r2r.at[other], dev(x, other, yc)).wait_recv()
    mine = jnp.sum(rs2[pl.ds(zh * NZL, NZL)], axis=0)
    theirs = jnp.sum(rs2[pl.ds((1 - zh) * NZL, NZL)], axis=0)
    rewards = mine + jnp.where(top == 0, theirs[1:2], jnp.where(top == 1, theirs[0:1], 0.0))

    margin = dot3(rewards, pairs)
    slope = 1.0 / (1.0 + jnp.exp(margin))
    dreward = -dot3(slope, onehot, NT)
    vrows = []
    for r in range(2):
        half = slice(r * RANK, (r + 1) * RANK)
        dscore = jnp.sum(maskv[...] * dreward[r : r + 1], axis=1, keepdims=True)
        qa[:, half] = (dscore * apre[:, half]).astype(BF16)
        qb[0:ROWS, half] = (dscore * cpre[:, half]).astype(BF16)
        vrows.append(jnp.sum(dscore * vpre[:, half], axis=0, keepdims=True))
    arow2 = lax.broadcasted_iota(I32, (AUG, RANK), 0)
    for r in range(2):
        hi, lo = split(vrows[r])
        tile = jnp.where((arow2 == 3 * r) | (arow2 == 3 * r + 2), hi.astype(F32), 0.0)
        tile = jnp.where(arow2 == 3 * r + 1, lo.astype(F32), tile)
        qb[ROWS : ROWS + AUG, r * RANK : (r + 1) * RANK] = tile.astype(BF16)
    mbd[...] = jnp.where(same, dot(lows[...], qb[0:ROWS, :], TN), 0.0).astype(BF16)

    def feature_chunk(k):
        return lax.rem(zl + OFFSETS[k], NZL)

    def target(u):
        return lax.rem(z + UNITS[u][1] + NZ, NZ)

    def place_of(u):
        half = lax.div(target(u), NZL)
        return UNITS[u][0], jnp.where(half == zh, 0, 1)

    places = [place_of(u) for u in range(len(UNITS))]

    def c1copy(u):
        return remote(gr.at[places[u]], rc.at[places[u]], c1s.at[u], c1r.at[u], core_peer)

    def spread(k, tmp, n, rows):
        for d in range(NY):
            own = tmp[pl.ds(pl.multiple_of((2 * d + c) * n, 16), n), :]
            other = tmp[pl.ds(pl.multiple_of((2 * d + 1 - c) * n, 16), n), :].astype(BF16)
            for r in range(2):
                g32[k, r, d, rows, :] = own[:, r * RANK : (r + 1) * RANK]
                gr[k, r, d, rows, :] = other[:, r * RANK : (r + 1) * RANK]

    def terms(k):
        j = feature_chunk(k)
        for i in range(4):
            cols = pl.ds(pl.multiple_of(j * 1024 + i * 256, 256), 256)
            tmpa[i * 256 : (i + 1) * 256, :] = dot(xa[:, cols], qa[...], TN)
        spread(k, tmpa, RA, slice(0, RA))
        for i in range(3):
            first = j * 1152 + i * 384
            cols = pl.ds(pl.multiple_of(first, 128), 384)
            tmpb[i * 384 : (i + 1) * 384, :] = dot(xb[:, cols], qb[...], TN) + dot(
                wcat(WA + first, 384), mbd[...]
            )
        spread(k, tmpb, RB, slice(RA, RAB))

    ya = y + 1 - 2 * lax.rem(y, 2)
    yb = 3 - y
    cut = (slice(0, RA), slice(RA, RAB))

    def flip(v):
        return v + 1 - 2 * lax.rem(v, 2)

    def sent1(p, i):
        to = (ya, yb)[p]
        return to if i == 0 else ((3 - to) if p == 0 else flip(to))

    def ycopy1(u, p):
        return remote(
            (b1a, b1b)[p].at[u], (s2a, s2b)[p].at[u],
            y1s.at[u, p], y1r.at[u, p], dev(x, z, (ya, yb)[p] * NC + c),
        )

    def ycopy2(u, p):
        buf = (sa, sb)[p]
        return remote(
            buf.at[0, u], buf.at[1, u], y2s.at[u, p], y2r.at[u, p], dev(x, z, (yb, ya)[p] * NC + c)
        )

    def fcopy(u):
        return remote(b2.at[u], fin.at[z], fs.at[u], fr.at[z], dev(x, target(u), yc))

    def coresum(u, p, chunk):
        k, r = places[u]
        return g32[k, r, chunk, cut[p], :] + rc[k, r, chunk, cut[p], :].astype(F32)

    def step1(u):
        c1copy(u).wait_recv()
        for p in range(2):
            for i in range(2):
                (b1a, b1b)[p][u, i] = coresum(u, p, sent1(p, i)).astype(BF16)
            ycopy1(u, p).start()

    def kept(u, p, chunk, i):
        return coresum(u, p, chunk) + (s2a, s2b)[p][u, i].astype(F32)

    def step2(u):
        for p in range(2):
            ycopy1(u, p).wait_recv()
            (sa, sb)[p][0, u] = kept(u, p, (yb, ya)[p], 1).astype(BF16)
            ycopy2(u, p).start()

    def sent(u):
        c1copy(u).wait_send()
        for p in range(2):
            ycopy1(u, p).wait_send()
            ycopy2(u, p).wait_send()
        if UNITS[u][1] != 0:
            fcopy(u).wait_send()

    def step3(u):
        for p in range(2):
            ycopy2(u, p).wait_recv()
            total = kept(u, p, y, 0) + (sa, sb)[p][1, u].astype(F32)
            b2[u, cut[p], :] = total.astype(BF16)
        if UNITS[u][1] == 0:
            fin[z] = b2[u]
        else:
            fcopy(u).start()

    terms(0)
    c1copy(0).start()
    for u in range(len(UNITS) + 4):
        if u + 1 < NZL:
            terms(u + 1)
            c1copy(u + 1).start()
        if u + 1 == NZL - 1:
            for later in range(NZL, len(UNITS)):
                c1copy(later).start()
        if u < len(UNITS):
            step1(u)
        if 2 <= u < len(UNITS) + 2:
            step2(u - 2)
        if u >= 4:
            step3(u - 4)
        if u >= 5:
            sent(u - 5)
        if u == len(UNITS) // 2:
            for copy in sends1 + sends2:
                copy.wait_send()
            soft = jnp.log1p(jnp.exp(-jnp.abs(margin))) + jnp.maximum(-margin, 0.0)
            loss = jnp.sum(jnp.where(even8 & (top == 0), soft, 0.0)) * (2.0 / RESP)
    for d in range(1, NZ):
        other = lax.rem(z + d, NZ)
        remote(b2.at[0], fin.at[other], fs.at[0], fr.at[other], dev(x, other, yc)).wait_recv()
    total = fin[0].astype(F32)
    for i in range(1, NZ):
        total = total + fin[i].astype(F32)
    out_ref[0:RAB, :] = total
    out_ref[RAB : RAB + 8, :] = jnp.full((8, RANK), loss, F32)

    sent(len(UNITS) - 1)


def divide(whole, loss, ga, gb):
    ga[0] = whole[0:RA]
    gb[0] = whole[RA:RAB]
    loss[0] = jnp.max(whole[RAB : RAB + 8])


def per_device(acts, base, down_matrices, up_matrices, head, gain, lengths, pairing):
    hbm = pl.BlockSpec(memory_space=pltpu.HBM)
    vmem = pl.BlockSpec(memory_space=pltpu.VMEM)
    smem = pl.BlockSpec(memory_space=pltpu.SMEM)
    dma = pltpu.SemaphoreType.DMA
    whole = pl.pallas_call(
        kernel,
        out_shape=jax.ShapeDtypeStruct((RAB + 8, RANK), F32),
        in_specs=[hbm] * 8,
        out_specs=vmem,
        scratch_shapes=[
            pltpu.VMEM((ROWS, WA), BF16),
            pltpu.VMEM((ROWS + AUG, WB), BF16),
            pltpu.VMEM((2, WAB, RANK), BF16),
            pltpu.VMEM((1, WB), BF16),
            pltpu.VMEM((WB // 128, 128), F32),
            pltpu.SMEM((1, 4), I32),
            pltpu.VMEM((1, RESP), I32),
            pltpu.VMEM((40, 128), F32),
            pltpu.VMEM((40, 128), F32),
            pltpu.VMEM((ROWS, RESP), F32),
            pltpu.VMEM((ROWS, 2 * RANK), F32),
            pltpu.VMEM((ROWS, 2 * RANK), F32),
            pltpu.VMEM((ROWS, 2 * RANK), F32),
            pltpu.VMEM((NY * NC, 8, RESP), F32),
            pltpu.VMEM((NZ, 8, RESP), F32),
            pltpu.VMEM((ROWS, 2 * RANK), BF16),
            pltpu.VMEM((ROWS, 2 * RANK), BF16),
            pltpu.VMEM((ROWS + AUG, 2 * RANK), BF16),
            pltpu.VMEM((2 * RANK, 2 * RANK), BF16),
            pltpu.VMEM((WA // NZL, 2 * RANK), F32),
            pltpu.VMEM((WB // NZL, 2 * RANK), F32),
            pltpu.VMEM((NZL, 2, NY, RAB, RANK), F32),
            pltpu.VMEM((NZL, 2, NY, RAB, RANK), BF16),
            pltpu.VMEM((NZL, 2, NY, RAB, RANK), BF16),
            pltpu.VMEM((2 * NZL, 2, RA, RANK), BF16),
            pltpu.VMEM((2 * NZL, 2, RB, RANK), BF16),
            pltpu.VMEM((2 * NZL, 2, RA, RANK), BF16),
            pltpu.VMEM((2 * NZL, 2, RB, RANK), BF16),
            pltpu.VMEM((2, 2 * NZL, RA, RANK), BF16),
            pltpu.VMEM((2, 2 * NZL, RB, RANK), BF16),
            pltpu.VMEM((2 * NZL, RAB, RANK), BF16),
            pltpu.VMEM((NZ, RAB, RANK), BF16),
            dma((8,)),
            dma((3, XP)),
            dma((3, XP)),
            dma((WCH,)),
            dma((WCH,)),
            dma((NY, WCH)),
            dma((NY, WCH)),
            dma((NY, WCH)),
            dma((NY, WCH)),
            dma,
            dma,
            dma((NY * NC,)),
            dma((NY * NC,)),
            dma((NZ,)),
            dma((NZ,)),
            dma((2 * NZL,)),
            dma((2 * NZL,)),
            dma((2 * NZL, 2)),
            dma((2 * NZL, 2)),
            dma((2 * NZL, 2)),
            dma((2 * NZL, 2)),
            dma((2 * NZL,)),
            dma((NZ,)),
        ],
        compiler_params=pltpu.CompilerParams(
            collective_id=0, has_side_effects=True, vmem_limit_bytes=60 * 1024 * 1024
        ),
    )(
        acts, base, down_matrices, up_matrices, head,
        gain.reshape(WB // 128, 128), lengths, pairing.reshape(1, RESP),
    )
    return pl.pallas_call(
        divide,
        out_shape=(
            jax.ShapeDtypeStruct((1,), F32),
            jax.ShapeDtypeStruct((1, RA, RANK), F32),
            jax.ShapeDtypeStruct((1, RB, RANK), F32),
        ),
        in_specs=[vmem],
        out_specs=(smem, vmem, vmem),
    )(whole)


def solution(mesh):
    return jax.shard_map(
        per_device,
        mesh=mesh,
        in_specs=(
            P("dp", "member", None, None),
            P("dp", "member", None, None),
            P("member", None, None),
            P("member", None, None),
            P("member", None),
            P(),
            P("dp", None),
            P(),
        ),
        out_specs=(P("member"), P("member", "dp", None), P("member", "dp", None)),
        check_vma=False,
    )
```
